32 devices in a mesh: rad: 8 (over z, y), ang: 4 (over x, core).
Axes of the slice: x: 2, y: 2, z: 4, core: 2. Of those that a mesh axis runs over, the one named last changes fastest.
Arguments:
- nonlin: bfloat16 [2, 512, 32768], P(None, 'rad', 'ang'), may hold values from -6 to 6
- state: float32 [2, 512, 32768], P(None, 'rad', 'ang'), may hold values from -6 to 6
- inverse: float32 [32, 2, 1024, 1024], P(('ang', 'rad')), may hold values from -0.1875 to 0.1875
- pair_of_slot: int32 [32], P(('ang', 'rad')), may hold values from 0 to 31, each once
Outputs:
- new_state: float32 [2, 512, 32768], P(None, 'rad', 'ang')
The draws below stay inside these ranges and needn't reach their ends.
Inputs may be any that keep to these rules, and one draw needn't show every extreme that they name: Slot s of the window holds degrees pair_of_slot[s] and 511 - pair_of_slot[s]; every pair once.
All inputs are finite; a program needn't handle non-finite values.
Results may differ from the reference program's by a relative error of at most 0.0003.
Values may be sent and summed in bfloat16 or wider, within the bound.
No kernel may reach another device: no remote copies, remote signals or barrier semaphores. Data moves between devices by JAX's collectives and lax.ppermute only.
A program may use at most 128 MiB of HBM per device.

```python
import math
import jax
import jax.numpy as jnp
from jax import lax

LMAX = 511
NR = 512
NPAIR = 32
NCOL = 32768


def levels(own_key, shape, split, smallest, top_value):
    def one(position, parts):
        draws = jax.random.uniform(jax.random.fold_in(jax.random.fold_in(own_key, 6), position), (parts,), jnp.float32, smallest / len(split), top_value / len(split))
        return jnp.repeat(jnp.exp(draws), shape[position] // parts).reshape((-1,) + (1,) * (len(shape) - position - 1))

    factor_of = one(*split[0])
    for cut in split[1:]:
        factor_of = factor_of * one(*cut)
    return factor_of


def bell_draw(rng, shape, width, bound, pieces=(), kind=jnp.bfloat16):
    loudness = levels(rng, shape, pieces, -0.22, 0.18) if pieces else 1.0
    result = jax.random.normal(rng, shape, jnp.float32) * width * loudness
    return jnp.minimum(jnp.maximum(result, -bound), bound).astype(kind)


def setup_inputs(seed: int = 0) -> dict:
    splits = jax.random.split(jax.random.key(seed), 5)
    nonlin = bell_draw(splits[0], (2, NR, NCOL), 1.0, 6.0, ((1, 8), (2, 4)))
    state = bell_draw(splits[1], (2, NR, NCOL), 1.0, 6.0, ((1, 8), (2, 4)), jnp.float32)
    inverse = bell_draw(splits[2], (NPAIR, 2, 2 * NR, 2 * NR), (2 * NR) ** -0.5, 0.1875, ((0, 32),), jnp.float32)
    pair_of_slot = jax.random.permutation(splits[3], NPAIR).astype(jnp.int32)
    return {"nonlin": nonlin, "state": state, "inverse": inverse, "pair_of_slot": pair_of_slot}


inner_radius = 0.35
outer_radius = 1.0
blend_weight = 0.5


def radius_at(level_index, total_levels):
    scaled = level_index / (total_levels - 1.0)
    stretch = (1.0 - blend_weight) * scaled + blend_weight * (1.0 - jnp.cos(math.pi * scaled)) / 2.0
    return inner_radius + (outer_radius - inner_radius) * stretch


def forcing(padded, old_state, first_level, total_levels):
    count = padded.shape[1] - 2
    values = padded.astype(jnp.float32)
    level_index = jnp.arange(count, dtype=jnp.float32) + first_level
    radius_here = radius_at(level_index, total_levels)
    step_below = radius_here - radius_at(level_index - 1.0, total_levels)
    step_above = radius_at(level_index + 1.0, total_levels) - radius_here
    at_inner = level_index == 0.0
    at_outer = level_index == total_levels - 1.0
    weight_below = jnp.where(at_inner, 0.0, jnp.where(at_outer, -1.0 / step_below, -step_above / (step_below * (step_below + step_above))))
    weight_here = jnp.where(at_inner, -1.0 / step_above, jnp.where(at_outer, 1.0 / step_below, (step_above - step_below) / (step_below * step_above)))
    weight_above = jnp.where(at_inner, 1.0 / step_above, jnp.where(at_outer, 0.0, step_below / (step_above * (step_below + step_above))))
    centre = values[:, 1:-1]
    derivative = weight_below[None, :, None] * values[:, :-2] + weight_here[None, :, None] * centre + weight_above[None, :, None] * values[:, 2:]
    time_step = 0.5 * (outer_radius - inner_radius) / (total_levels - 1.0)
    return old_state + time_step * (derivative + 2.0 * centre / radius_here[None, :, None])


def lower_mask(column_count, pair_index):
    half_cols = column_count // 2
    column_index = jnp.arange(column_count, dtype=jnp.int32)
    first_half = column_index < pair_index + 1
    second_half = (column_index >= half_cols) & (column_index - half_cols < pair_index)
    return jnp.where(column_index < half_cols, first_half, second_half)


def apply_inverse(block, matrices, pair_index):
    field_count, level_count, column_count = block.shape
    flattened = block.reshape(field_count * level_count, column_count)
    lower_part = jnp.dot(matrices[0], flattened, precision=lax.Precision.HIGHEST, preferred_element_type=jnp.float32)
    upper_part = jnp.dot(matrices[1], flattened, precision=lax.Precision.HIGHEST, preferred_element_type=jnp.float32)
    chosen = jnp.where(lower_mask(column_count, pair_index)[None, :], lower_part, upper_part)
    return chosen.reshape(field_count, level_count, column_count)


def reference(nonlin, state, inverse, pair_of_slot):
    level_count = nonlin.shape[1]
    padded = jnp.pad(nonlin, ((0, 0), (1, 1), (0, 0)))
    right_side = forcing(padded, state, jnp.float32(0.0), level_count * 1.0)
    column_count = 2 * (LMAX + 1)
    slot_count = right_side.shape[2] // column_count
    blocks = right_side.reshape(2, level_count, slot_count, column_count).transpose(2, 0, 1, 3)

    def one_slot(packed):
        block, matrices, pair_index = packed
        return apply_inverse(block, matrices, pair_index)

    solved = lax.map(one_slot, (blocks, inverse, pair_of_slot))
    return solved.transpose(1, 2, 0, 3).reshape(2, level_count, slot_count * column_count)
```

```python
import functools
import math

import jax
import jax.numpy as jnp
import numpy as np
from jax import lax
from jax.experimental import pallas as pl
from jax.experimental.pallas import tpu as pltpu
from jax.sharding import PartitionSpec as P

inner_radius = 0.35
outer_radius = 1.0
blend_weight = 0.5

LANES = 128
TILE = 16
CHUNKS = 2
TOP = 32700.0
FINE = 128.0
MIB = 1024 * 1024


def radius_at(level_index, total_levels):
    scaled = level_index / (total_levels - 1.0)
    stretch = (1.0 - blend_weight) * scaled + blend_weight * (1.0 - np.cos(math.pi * scaled)) / 2.0
    return inner_radius + (outer_radius - inner_radius) * stretch


def stencil_table(total_levels):
    k = np.arange(total_levels, dtype=np.float64)
    radius = radius_at(k, total_levels)
    below = radius - radius_at(k - 1.0, total_levels)
    above = radius_at(k + 1.0, total_levels) - radius
    at_inner, at_outer = k == 0, k == total_levels - 1
    weight_below = np.where(at_inner, 0.0, np.where(at_outer, -1.0 / below, -above / (below * (below + above))))
    weight_here = np.where(
        at_inner, -1.0 / above, np.where(at_outer, 1.0 / below, (above - below) / (below * above))
    )
    weight_above = np.where(at_inner, 1.0 / above, np.where(at_outer, 0.0, below / (above * (below + above))))
    time_step = 0.5 * (outer_radius - inner_radius) / (total_levels - 1.0)
    table = np.zeros((total_levels, LANES), np.float32)
    table[:, 0] = time_step * weight_below
    table[:, 1] = time_step * (weight_here + 2.0 / radius)
    table[:, 2] = time_step * weight_above
    return table


def scale_code(values):
    largest = jnp.maximum(jnp.max(jnp.abs(values), axis=0, keepdims=True), 1e-30)
    return jnp.ceil(jnp.log2(largest) * FINE)


def encode(values, code):
    scaled = values * (jnp.exp2(code * (-1.0 / FINE)) * TOP)
    scaled = jnp.clip(jnp.round(scaled), -32767.0, 32767.0)
    return scaled.astype(jnp.int32).astype(jnp.int16)


def scale_of(codes):
    return jnp.exp2(codes.astype(jnp.int32).astype(jnp.float32) * (1.0 / FINE)) * (1.0 / TOP)


def pack_codes(codes):
    rows = codes + [jnp.zeros_like(codes[0])] * (TILE - len(codes))
    return jnp.concatenate(rows, axis=0).astype(jnp.int32).astype(jnp.int16)


def right_side_kernel(groups, slabs, where, n_ref, s_ref, before_ref, after_ref, tab_ref, *rest):
    outs, buffer = rest[:groups], rest[groups]
    levels = n_ref.shape[1]
    rows = 2 * levels
    step = pl.program_id(0)
    tab = tab_ref[...]
    below, here, above = (jnp.broadcast_to(tab[:, i : i + 1], (levels, LANES)) for i in range(3))
    row = lax.broadcasted_iota(jnp.int32, (levels, LANES), 0)
    codes = []
    for slab in range(slabs):
        cols = slice(slab * LANES, (slab + 1) * LANES)
        fields = []
        for f in range(2):
            n = n_ref[f, :, cols].astype(jnp.float32)
            prev = jnp.where(row == 0, before_ref[f, :, cols].astype(jnp.float32), pltpu.roll(n, 1, 0))
            succ = jnp.where(
                row == levels - 1, after_ref[f, :, cols].astype(jnp.float32), pltpu.roll(n, levels - 1, 0)
            )
            fields.append(s_ref[f, :, cols] + (below * prev + here * n + above * succ))
        both = jnp.concatenate(fields, axis=0)
        code = scale_code(both)
        codes.append(code)
        buffer[slab * rows : (slab + 1) * rows, :] = encode(both, code)
    buffer[slabs * rows :, :] = pack_codes(codes)
    for k in range(groups):

        @pl.when(step == k)
        def _():
            outs[k][...] = buffer[...]


def split_kernel(a_ref, hi_ref, lo_ref):
    a = a_ref[...]
    hi = a.astype(jnp.bfloat16)
    hi_ref[...] = hi
    lo_ref[...] = (a - hi.astype(jnp.float32)).astype(jnp.bfloat16)


def product_kernel(groups, slabs, lower_slabs, first_col, half_cols, where, *refs):
    ins, (hi_ref, lo_ref), outs = refs[:groups], refs[groups : groups + 2], refs[groups + 2 : 2 * groups + 2]
    v_hi, v_lo, y = refs[2 * groups + 2 :]
    size = y.shape[0]
    levels = size // (2 * groups)
    rows = 2 * levels
    me = where[0]
    pair = where[1]
    for k in range(groups):
        peer = lax.bitwise_xor(me, k)
        scales = scale_of(ins[k][slabs * rows :, :])
        for slab in range(slabs):
            cols = slice(slab * LANES, (slab + 1) * LANES)
            for f in range(2):
                at = slab * rows + f * levels
                v = ins[k][at : at + levels, :].astype(jnp.int32).astype(jnp.float32) * scales[slab : slab + 1, :]
                to = pl.ds(pl.multiple_of(f * (size // 2) + peer * levels, levels), levels)
                hi = v.astype(jnp.bfloat16)
                v_hi[to, cols] = hi
                v_lo[to, cols] = (v - hi.astype(jnp.float32)).astype(jnp.bfloat16)

    def product(which, cols):
        dot = functools.partial(jnp.dot, preferred_element_type=jnp.float32)
        return (
            dot(lo_ref[which], v_hi[:, cols])
            + dot(hi_ref[which], v_lo[:, cols])
            + dot(hi_ref[which], v_hi[:, cols])
        )

    wide = min(2 * LANES, slabs * LANES)
    for at in range(0, slabs * LANES, wide):
        y[:, at : at + wide] = product(1, slice(at, at + wide))
    for slab in range(slabs):
        first = first_col + slab * LANES
        if first % half_cols < lower_slabs * LANES:
            cols = slice(slab * LANES, (slab + 1) * LANES)
            column = first % half_cols + lax.broadcasted_iota(jnp.int32, (size, LANES), 1)
            bound = pair + 1 if first < half_cols else pair
            y[:, cols] = jnp.where(column < bound, product(0, cols), y[:, cols])

    for k in range(groups):
        peer = lax.bitwise_xor(me, k)
        codes = []
        for slab in range(slabs):
            cols = slice(slab * LANES, (slab + 1) * LANES)
            both = jnp.concatenate(
                [
                    y[pl.ds(pl.multiple_of(f * (size // 2) + peer * levels, levels), levels), cols]
                    for f in range(2)
                ],
                axis=0,
            )
            code = scale_code(both)
            codes.append(code)
            outs[k][slab * rows : (slab + 1) * rows, :] = encode(both, code)
        outs[k][slabs * rows :, :] = pack_codes(codes)


def result_kernel(groups, slabs, where, *refs):
    ins, out_ref = refs[:groups], refs[-1]
    levels = out_ref.shape[1]
    rows = 2 * levels
    step = pl.program_id(0)
    for k in range(groups):

        @pl.when(step == k)
        def _():
            scales = scale_of(ins[k][slabs * rows :, :])
            for slab in range(slabs):
                for f in range(2):
                    at = slab * rows + f * levels
                    v = ins[k][at : at + levels, :].astype(jnp.int32).astype(jnp.float32)
                    out_ref[f, :, slab * LANES : (slab + 1) * LANES] = v * scales[slab : slab + 1, :]


def exchange(messages, groups):
    got = list(messages)
    for k in reversed(range(1, groups)):
        got[k] = lax.ppermute(messages[k], "rad", [(i, i ^ k) for i in range(groups)])
    return got


def neighbours(nonlin, groups):
    up = [(i, i + 1) for i in range(groups - 1)]
    down = [(j, i) for i, j in up]
    before = lax.ppermute(nonlin[:, -1:, :], "rad", up)
    after = lax.ppermute(nonlin[:, :1, :], "rad", down)
    return before, after


def local(slots, nonlin, state, inverse, pair_of_slot):
    levels = nonlin.shape[1]
    groups = lax.axis_size("rad")
    width = nonlin.shape[2] // groups
    size = inverse.shape[-1]
    span = width // CHUNKS
    slabs = span // LANES
    rows = 2 * levels
    lower_slabs = -(-slots // LANES)
    me = lax.axis_index("rad").astype(jnp.int32)
    where = jnp.stack([me, pair_of_slot[0].astype(jnp.int32)])
    table = jnp.asarray(stencil_table(levels * groups))
    message = jax.ShapeDtypeStruct((slabs * rows + TILE, LANES), jnp.int16)
    whole = pl.BlockSpec(message.shape, lambda *_: (0, 0))
    vmem = pl.BlockSpec(memory_space=pltpu.VMEM)
    before, after = neighbours(nonlin, groups)

    def right_side(chunk):
        def at(k, w):
            return (0, 0, lax.bitwise_xor(w[0], k) * CHUNKS + chunk)

        return pl.pallas_call(
            functools.partial(right_side_kernel, groups, slabs),
            out_shape=[message] * groups,
            grid_spec=pltpu.PrefetchScalarGridSpec(
                num_scalar_prefetch=1,
                grid=(groups,),
                in_specs=[
                    pl.BlockSpec((2, levels, span), at),
                    pl.BlockSpec((2, levels, span), at),
                    pl.BlockSpec((2, 1, span), at),
                    pl.BlockSpec((2, 1, span), at),
                    pl.BlockSpec((levels, LANES), lambda k, w: (w[0], 0)),
                ],
                out_specs=[whole] * groups,
                scratch_shapes=[pltpu.VMEM(message.shape, jnp.int16)],
            ),
            compiler_params=pltpu.CompilerParams(vmem_limit_bytes=16 * MIB),
            cost_estimate=pl.CostEstimate(flops=4 * MIB, bytes_accessed=4 * MIB, transcendentals=0),
            name="right_side",
        )(where, nonlin, state, before, after, table)

    def split():
        block = pl.BlockSpec((1, size // 4, size), lambda i, j: (i, j, 0))
        half = jax.ShapeDtypeStruct((2, size, size), jnp.bfloat16)
        return pl.pallas_call(
            split_kernel,
            out_shape=[half, half],
            grid=(2, 4),
            in_specs=[block],
            out_specs=[block, block],
            compiler_params=pltpu.CompilerParams(vmem_limit_bytes=16 * MIB),
            cost_estimate=pl.CostEstimate(flops=4 * MIB, bytes_accessed=16 * MIB, transcendentals=0),
            name="split_inverse",
        )(inverse[0])

    def product(chunk, messages, hi, lo):
        return pl.pallas_call(
            functools.partial(product_kernel, groups, slabs, lower_slabs, chunk * span, width // 2),
            out_shape=[message] * groups,
            grid_spec=pltpu.PrefetchScalarGridSpec(
                num_scalar_prefetch=1,
                grid=(),
                in_specs=[vmem] * (groups + 2),
                out_specs=[vmem] * groups,
                scratch_shapes=[
                    pltpu.VMEM((size, span), jnp.bfloat16),
                    pltpu.VMEM((size, span), jnp.bfloat16),
                    pltpu.VMEM((size, span), jnp.float32),
                ],
            ),
            compiler_params=pltpu.CompilerParams(vmem_limit_bytes=32 * MIB),
            cost_estimate=pl.CostEstimate(
                flops=6 * size * size * span, bytes_accessed=10 * MIB, transcendentals=0
            ),
            name="product",
        )(where, *messages, hi, lo)

    def result(chunk, messages, previous):
        def at(k, w):
            return (0, 0, lax.bitwise_xor(w[0], k) * CHUNKS + chunk)

        out_shape = jax.ShapeDtypeStruct(state.shape, jnp.float32)
        carried = [] if previous is None else [previous]
        return pl.pallas_call(
            functools.partial(result_kernel, groups, slabs),
            out_shape=out_shape,
            grid_spec=pltpu.PrefetchScalarGridSpec(
                num_scalar_prefetch=1,
                grid=(groups,),
                in_specs=[whole] * groups + [pl.BlockSpec(memory_space=pl.ANY)] * len(carried),
                out_specs=pl.BlockSpec((2, levels, span), at),
            ),
            input_output_aliases={} if previous is None else {groups + 1: 0},
            compiler_params=pltpu.CompilerParams(vmem_limit_bytes=16 * MIB),
            cost_estimate=pl.CostEstimate(flops=MIB, bytes_accessed=3 * MIB, transcendentals=0),
            name="result",
        )(where, *messages, *carried)

    sent = [exchange(right_side(c), groups) for c in range(CHUNKS)]
    hi, lo = split()
    back = [exchange(product(c, sent[c], hi, lo), groups) for c in range(CHUNKS)]
    out = None
    for c in range(CHUNKS):
        out = result(c, back[c], out)
    return out


def solution(mesh):
    placed = (
        P(None, "rad", "ang"),
        P(None, "rad", "ang"),
        P(("ang", "rad"), None, None, None),
        P(("ang", "rad")),
    )
    slots = mesh.shape["rad"] * mesh.shape["ang"]
    return jax.shard_map(
        functools.partial(local, slots),
        mesh=mesh,
        in_specs=placed,
        out_specs=P(None, "rad", "ang"),
        check_vma=False,
    )
```

```python
import functools
import math

import jax
import jax.numpy as jnp
import numpy as np
from jax import lax
from jax.experimental import pallas as pl
from jax.experimental.pallas import tpu as pltpu
from jax.sharding import PartitionSpec as P

inner_radius = 0.35
outer_radius = 1.0
blend_weight = 0.5

LANES = 128
TILE = 16
CHUNKS = 2
TOP = 32700.0
EDGE_TOP = 16384.0
FINE = 128.0
MIB = 1024 * 1024


def radius_at(level_index, total_levels):
    scaled = level_index / (total_levels - 1.0)
    stretch = (1.0 - blend_weight) * scaled + blend_weight * (1.0 - np.cos(math.pi * scaled)) / 2.0
    return inner_radius + (outer_radius - inner_radius) * stretch


def stencil_table(total_levels):
    k = np.arange(total_levels, dtype=np.float64)
    radius = radius_at(k, total_levels)
    below = radius - radius_at(k - 1.0, total_levels)
    above = radius_at(k + 1.0, total_levels) - radius
    at_inner, at_outer = k == 0, k == total_levels - 1
    weight_below = np.where(at_inner, 0.0, np.where(at_outer, -1.0 / below, -above / (below * (below + above))))
    weight_here = np.where(
        at_inner, -1.0 / above, np.where(at_outer, 1.0 / below, (above - below) / (below * above))
    )
    weight_above = np.where(at_inner, 1.0 / above, np.where(at_outer, 0.0, below / (above * (below + above))))
    time_step = 0.5 * (outer_radius - inner_radius) / (total_levels - 1.0)
    table = np.zeros((total_levels, LANES), np.float32)
    table[:, 0] = time_step * weight_below
    table[:, 1] = time_step * (weight_here + 2.0 / radius)
    table[:, 2] = time_step * weight_above
    return table


def scale_code(values, per_octave):
    largest = jnp.maximum(jnp.max(jnp.abs(values), axis=0, keepdims=True), 1e-30)
    return jnp.ceil(jnp.log2(largest) * per_octave) * (FINE / per_octave)


def encode(values, code, top):
    scaled = values * (jnp.exp2(code * (-1.0 / FINE)) * top)
    return jnp.clip(jnp.round(scaled), -32767.0, 32767.0)


def to_int16(values):
    return values.astype(jnp.int32).astype(jnp.int16)


def to_float(codes):
    return codes.astype(jnp.int32).astype(jnp.float32)


def scale_of(codes, top):
    return jnp.exp2(to_float(codes) * (1.0 / FINE)) * (1.0 / top)


def padded_rows(parts, rows):
    used = sum(p.shape[0] for p in parts)
    return jnp.concatenate(parts + [jnp.zeros((rows - used, LANES), jnp.float32)], axis=0)


def tile_rows(rows):
    return -(-rows // TILE) * TILE


def right_side_kernel(partners, parts, slabs, where, n_ref, s_ref, tab_ref, *outs):
    levels = n_ref.shape[1]
    rows = 2 * levels
    step = pl.program_id(0)
    tab = tab_ref[...]
    below, here, above = (jnp.broadcast_to(tab[:, i : i + 1], (levels, LANES)) for i in range(3))
    row = lax.broadcasted_iota(jnp.int32, (levels, LANES), 0)
    for at, _ in enumerate(partners):

        @pl.when(step == at)
        def _():
            for part in range(parts):
                codes, edge_codes, edges = [], [], []
                for slab in range(slabs):
                    cols = slice((part * slabs + slab) * LANES, (part * slabs + slab + 1) * LANES)
                    fields, ends = [], []
                    for f in range(2):
                        n = n_ref[f, :, cols].astype(jnp.float32)
                        prev = jnp.where(row == 0, n, pltpu.roll(n, 1, 0))
                        succ = jnp.where(row == levels - 1, n, pltpu.roll(n, levels - 1, 0))
                        fields.append(s_ref[f, :, cols] + (below * prev + here * n + above * succ))
                        ends += [n[:1], n[levels - 1 :]]
                    both = jnp.concatenate(fields, axis=0)
                    code = scale_code(both, FINE)
                    codes.append(code)
                    outs[at][part, slab * rows : (slab + 1) * rows, :] = to_int16(encode(both, code, TOP))
                    ends = jnp.concatenate(ends, axis=0)
                    code = scale_code(ends, 1.0)
                    edge_codes.append(code)
                    edges.append(encode(ends, code, EDGE_TOP))
                extra = outs[at].shape[1] - slabs * rows
                outs[at][part, slabs * rows :, :] = to_int16(padded_rows(edges + edge_codes + codes, extra))


def split_kernel(a_ref, hi_ref, lo_ref):
    a = a_ref[...]
    hi = a.astype(jnp.bfloat16)
    hi_ref[...] = hi
    lo_ref[...] = (a - hi.astype(jnp.float32)).astype(jnp.bfloat16)


def product_kernel(groups, slabs, lower_slabs, first_col, half_cols, places, carried, outs_at, where, edge_weight, *refs):
    ins, (hi_ref, lo_ref), refs = refs[:groups], refs[groups : groups + 2], refs[groups + 2 :]
    earlier, refs = refs[: len(carried)], refs[len(carried) :]
    outs, (v_hi, v_lo, y, edges) = refs[:groups], refs[groups:]
    size = y.shape[0]
    levels = size // (2 * groups)
    rows = 2 * levels
    me = where[0]
    pair = where[1]
    peers = [lax.bitwise_xor(me, k) for k in range(groups)]
    for k, ref in zip(carried, earlier):
        outs[k][: outs_at[k]] = ref[...]

    extra = []
    for k in range(groups):
        extra.append(ins[k][places[k], slabs * rows :, :])
        for slab in range(slabs):
            code = extra[k][4 * slabs + slab : 4 * slabs + slab + 1]
            edges[peers[k], :, slab * LANES : (slab + 1) * LANES] = to_float(
                extra[k][4 * slab : 4 * slab + 4]
            ) * scale_of(code, EDGE_TOP)
    near = lax.broadcasted_iota(jnp.int32, (8, LANES), 0)
    for k in range(groups):
        peer = peers[k]
        before, after = jnp.maximum(peer - 1, 0), jnp.minimum(peer + 1, groups - 1)
        weight_before, weight_after = edge_weight[peer], edge_weight[groups + peer]
        for slab in range(slabs):
            cols = slice(slab * LANES, (slab + 1) * LANES)
            scale = scale_of(extra[k][5 * slabs + slab : 5 * slabs + slab + 1], TOP)
            here = edges[peer, :, cols]
            low = weight_before * (edges[before, :, cols] - here_shifted(here))
            high = weight_after * (edges[after, :, cols] - here_shifted(here))
            for f in range(2):
                at = slab * rows + f * levels
                v = to_float(ins[k][places[k], at : at + levels, :]) * scale
                first = v[:8] + jnp.where(near == 0, low[2 * f + 1 : 2 * f + 2], 0.0)
                last = v[levels - 8 :] + jnp.where(near == 7, high[2 * f : 2 * f + 1], 0.0)
                middle = [v[8 : levels - 8]] if levels > 16 else []
                v = jnp.concatenate([first] + middle + [last], axis=0)
                to = pl.ds(pl.multiple_of(f * (size // 2) + peer * levels, levels), levels)
                hi = v.astype(jnp.bfloat16)
                v_hi[to, cols] = hi
                v_lo[to, cols] = (v - hi.astype(jnp.float32)).astype(jnp.bfloat16)

    def product(which, cols):
        dot = functools.partial(jnp.dot, preferred_element_type=jnp.float32)
        return (
            dot(lo_ref[which], v_hi[:, cols])
            + dot(hi_ref[which], v_lo[:, cols])
            + dot(hi_ref[which], v_hi[:, cols])
        )

    wide = min(2 * LANES, slabs * LANES)
    for at in range(0, slabs * LANES, wide):
        y[:, at : at + wide] = product(1, slice(at, at + wide))
    for slab in range(slabs):
        first = first_col + slab * LANES
        if first % half_cols < lower_slabs * LANES:
            cols = slice(slab * LANES, (slab + 1) * LANES)
            column = first % half_cols + lax.broadcasted_iota(jnp.int32, (size, LANES), 1)
            bound = pair + 1 if first < half_cols else pair
            y[:, cols] = jnp.where(column < bound, product(0, cols), y[:, cols])

    for k in range(groups):
        codes = []
        for slab in range(slabs):
            cols = slice(slab * LANES, (slab + 1) * LANES)
            both = jnp.concatenate(
                [
                    y[pl.ds(pl.multiple_of(f * (size // 2) + peers[k] * levels, levels), levels), cols]
                    for f in range(2)
                ],
                axis=0,
            )
            code = scale_code(both, FINE)
            codes.append(code)
            outs[k][outs_at[k], slab * rows : (slab + 1) * rows, :] = to_int16(encode(both, code, TOP))
        extra_rows = outs[k].shape[1] - slabs * rows
        outs[k][outs_at[k], slabs * rows :, :] = to_int16(padded_rows(codes, extra_rows))


def here_shifted(edges):
    return jnp.concatenate([edges[1:2], edges[0:1], edges[3:4], edges[2:3]], axis=0)


def result_kernel(count, parts, slabs, where, *refs):
    ins, out_ref = refs[:count], refs[-1]
    levels = out_ref.shape[1]
    rows = 2 * levels
    step = pl.program_id(0)
    for at in range(count):

        @pl.when(step == at)
        def _():
            for part in range(parts):
                scales = scale_of(ins[at][part, slabs * rows :, :], TOP)
                for slab in range(slabs):
                    for f in range(2):
                        first = slab * rows + f * levels
                        v = to_float(ins[at][part, first : first + levels, :]) * scales[slab : slab + 1, :]
                        out_ref[f, :, (part * slabs + slab) * LANES : (part * slabs + slab + 1) * LANES] = v


def send(message, k, groups):
    return message if k == 0 else lax.ppermute(message, "rad", [(i, i ^ k) for i in range(groups)])


def xor_block(ks, chunks, first_chunk):
    def at(step, w):
        k = jnp.int32(ks[-1])
        for i, value in enumerate(ks[:-1]):
            k = jnp.where(step == i, value, k)
        return (0, 0, lax.bitwise_xor(w[0], k) * chunks + first_chunk)

    return at


def local(slots, nonlin, state, inverse, pair_of_slot):
    levels = nonlin.shape[1]
    groups = lax.axis_size("rad")
    width = nonlin.shape[2] // groups
    size = inverse.shape[-1]
    span = width // CHUNKS
    slabs = span // LANES
    rows = 2 * levels
    lower_slabs = -(-slots // LANES)
    me = lax.axis_index("rad").astype(jnp.int32)
    where = jnp.stack([me, pair_of_slot[0].astype(jnp.int32)])
    weights = stencil_table(levels * groups)
    table = jnp.asarray(weights)
    edge_weight = jnp.asarray(np.concatenate([weights[::levels, 0], weights[levels - 1 :: levels, 2]]))
    out_rows = slabs * rows + tile_rows(6 * slabs)
    back_rows = slabs * rows + tile_rows(slabs)
    vmem = pl.BlockSpec(memory_space=pltpu.VMEM)
    hbm = pl.BlockSpec(memory_space=pl.ANY)
    far = list(range(groups // 2, groups))
    near = list(range(groups // 2))

    def right_side(ks, parts, first):
        at = xor_block(ks, CHUNKS // parts, first)
        shape = (parts, out_rows, LANES)
        return pl.pallas_call(
            functools.partial(right_side_kernel, ks, parts, slabs),
            out_shape=[jax.ShapeDtypeStruct(shape, jnp.int16)] * len(ks),
            grid_spec=pltpu.PrefetchScalarGridSpec(
                num_scalar_prefetch=1,
                grid=(len(ks),),
                in_specs=[
                    pl.BlockSpec((2, levels, parts * span), at),
                    pl.BlockSpec((2, levels, parts * span), at),
                    pl.BlockSpec((levels, LANES), lambda k, w: (w[0], 0)),
                ],
                out_specs=[pl.BlockSpec(shape, lambda k, w: (0, 0, 0))] * len(ks),
            ),
            compiler_params=pltpu.CompilerParams(vmem_limit_bytes=56 * MIB),
            cost_estimate=pl.CostEstimate(flops=4 * MIB, bytes_accessed=4 * MIB, transcendentals=0),
            name="right_side",
        )(where, nonlin, state, table)

    def split():
        block = pl.BlockSpec((1, size // 4, size), lambda i, j: (i, j, 0))
        half = jax.ShapeDtypeStruct((2, size, size), jnp.bfloat16)
        return pl.pallas_call(
            split_kernel,
            out_shape=[half, half],
            grid=(2, 4),
            in_specs=[block],
            out_specs=[block, block],
            compiler_params=pltpu.CompilerParams(vmem_limit_bytes=16 * MIB),
            cost_estimate=pl.CostEstimate(flops=4 * MIB, bytes_accessed=16 * MIB, transcendentals=0),
            name="split_inverse",
        )(inverse[0])

    def product(chunk, messages, places, hi, lo, carried, outs_at):
        shapes = [
            jax.ShapeDtypeStruct((outs_at[k] + 1, back_rows, LANES), jnp.int16) for k in range(groups)
        ]
        return pl.pallas_call(
            functools.partial(
                product_kernel,
                groups,
                slabs,
                lower_slabs,
                chunk * span,
                width // 2,
                places,
                tuple(carried),
                outs_at,
            ),
            out_shape=shapes,
            grid_spec=pltpu.PrefetchScalarGridSpec(
                num_scalar_prefetch=1,
                grid=(),
                in_specs=[pl.BlockSpec(memory_space=pltpu.SMEM)] + [vmem] * (groups + 2 + len(carried)),
                out_specs=[vmem] * groups,
                scratch_shapes=[
                    pltpu.VMEM((size, span), jnp.bfloat16),
                    pltpu.VMEM((size, span), jnp.bfloat16),
                    pltpu.VMEM((size, span), jnp.float32),
                    pltpu.VMEM((groups, 4, span), jnp.float32),
                ],
            ),
            compiler_params=pltpu.CompilerParams(vmem_limit_bytes=32 * MIB),
            cost_estimate=pl.CostEstimate(
                flops=6 * size * size * span, bytes_accessed=10 * MIB, transcendentals=0
            ),
            name="product",
        )(where, edge_weight, *messages, hi, lo, *carried.values())

    def result(ks, parts, first, messages, previous):
        at = xor_block(ks, CHUNKS // parts, first)
        out_shape = jax.ShapeDtypeStruct(state.shape, jnp.float32)
        carried = [] if previous is None else [previous]
        whole = [pl.BlockSpec(m.shape, lambda k, w: (0, 0, 0)) for m in messages]
        return pl.pallas_call(
            functools.partial(result_kernel, len(ks), parts, slabs),
            out_shape=out_shape,
            grid_spec=pltpu.PrefetchScalarGridSpec(
                num_scalar_prefetch=1,
                grid=(len(ks),),
                in_specs=whole + [hbm] * len(carried),
                out_specs=pl.BlockSpec((2, levels, parts * span), at),
            ),
            input_output_aliases={} if previous is None else {len(ks) + 1: 0},
            compiler_params=pltpu.CompilerParams(vmem_limit_bytes=16 * MIB),
            cost_estimate=pl.CostEstimate(flops=MIB, bytes_accessed=3 * MIB, transcendentals=0),
            name="result",
        )(where, *messages, *carried)

    plan = [(far, 1, 0), (near, CHUNKS, 0)] + [(far, 1, c) for c in range(1, CHUNKS)]
    got = {}
    for ks, parts, first in plan:
        for k, message in zip(ks, right_side(ks, parts, first)):
            arrived = send(message, k, groups)
            for c in range(first, first + parts):
                got[k, c] = (arrived, c - first)
    hi, lo = split()
    back, made = {}, {}
    for c in range(CHUNKS):
        messages, places = zip(*[got[k, c] for k in range(groups)])
        outs_at = [c if k in near else 0 for k in range(groups)]
        carried = {k: made[k] for k in near} if c else {}
        made = dict(enumerate(product(c, messages, places, hi, lo, carried, outs_at)))
        back.update({(k, c): send(made[k], k, groups) for k in far})
    back.update({(k, 0): send(made[k], k, groups) for k in near})
    out = None
    for ks, parts, first in [(far, 1, c) for c in range(CHUNKS - 1)] + [(near, CHUNKS, 0), (far, 1, CHUNKS - 1)]:
        out = result(ks, parts, first, [back[k, first] for k in ks], out)
    return out


def solution(mesh):
    placed = (
        P(None, "rad", "ang"),
        P(None, "rad", "ang"),
        P(("ang", "rad"), None, None, None),
        P(("ang", "rad")),
    )
    slots = mesh.shape["rad"] * mesh.shape["ang"]
    return jax.shard_map(
        functools.partial(local, slots),
        mesh=mesh,
        in_specs=placed,
        out_specs=P(None, "rad", "ang"),
        check_vma=False,
    )
```

```python
import functools
import math

import jax
import jax.numpy as jnp
import numpy as np
from jax import lax
from jax.experimental import pallas as pl
from jax.experimental.pallas import tpu as pltpu
from jax.sharding import PartitionSpec as P

inner_radius = 0.35
outer_radius = 1.0
blend_weight = 0.5

LANES = 128
TILE = 16
EXTRA = 8
SHARES = ((0, 4), (4, 4))
TOP = 32700.0
EDGE_TOP = 16384.0
FINE = 128.0
MIB = 1024 * 1024


def radius_at(level_index, total_levels):
    scaled = level_index / (total_levels - 1.0)
    stretch = (1.0 - blend_weight) * scaled + blend_weight * (1.0 - np.cos(math.pi * scaled)) / 2.0
    return inner_radius + (outer_radius - inner_radius) * stretch


def stencil_table(total_levels):
    k = np.arange(total_levels, dtype=np.float64)
    radius = radius_at(k, total_levels)
    below = radius - radius_at(k - 1.0, total_levels)
    above = radius_at(k + 1.0, total_levels) - radius
    at_inner, at_outer = k == 0, k == total_levels - 1
    weight_below = np.where(at_inner, 0.0, np.where(at_outer, -1.0 / below, -above / (below * (below + above))))
    weight_here = np.where(
        at_inner, -1.0 / above, np.where(at_outer, 1.0 / below, (above - below) / (below * above))
    )
    weight_above = np.where(at_inner, 1.0 / above, np.where(at_outer, 0.0, below / (above * (below + above))))
    time_step = 0.5 * (outer_radius - inner_radius) / (total_levels - 1.0)
    table = np.zeros((total_levels, LANES), np.float32)
    table[:, 0] = time_step * weight_below
    table[:, 1] = time_step * (weight_here + 2.0 / radius)
    table[:, 2] = time_step * weight_above
    return table


def scale_code(largest, per_octave):
    return jnp.ceil(jnp.log2(jnp.maximum(largest, 1e-30)) * per_octave) * (FINE / per_octave)


def encode_factor(code, top):
    return jnp.exp2(code * (-1.0 / FINE)) * top


def to_int16(values):
    return values.astype(jnp.int32).astype(jnp.int16)


def to_float(codes):
    return codes.astype(jnp.int32).astype(jnp.float32)


def scale_of(codes, top):
    return jnp.exp2(codes * (1.0 / FINE)) * (1.0 / top)


def lanes_of(slab):
    return pl.ds(pl.multiple_of(slab * LANES, LANES), LANES)


def right_side_kernel(slabs, partners, where, n_ref, s_ref, tab_ref, *refs):
    outs, (buffer, values, tops, extra) = refs[-4 - partners : -4], refs[-4:]
    levels = n_ref.shape[1]
    rows = 2 * levels
    tab = tab_ref[...]
    below, here, above = (jnp.broadcast_to(tab[:, i : i + 1], (levels, LANES)) for i in range(3))
    row = lax.broadcasted_iota(jnp.int32, (levels, LANES), 0)

    def rows_of(slab):
        return pl.ds(pl.multiple_of(slab * rows, rows), rows)

    def compute(slab, _):
        ends, top = [], jnp.zeros((8, LANES), jnp.float32)
        for f in range(2):
            n = n_ref[f, :, lanes_of(slab)].astype(jnp.float32)
            prev = jnp.where(row == 0, n, pltpu.roll(n, 1, 0))
            succ = jnp.where(row == levels - 1, n, pltpu.roll(n, levels - 1, 0))
            v = s_ref[f, :, lanes_of(slab)] + (below * prev + here * n + above * succ)
            values[pl.ds(pl.multiple_of(slab * rows + f * levels, levels), levels), :] = v
            top = jnp.maximum(top, jnp.max(jnp.abs(v).reshape(levels // 8, 8, LANES), axis=0))
            ends += [n[:1], n[levels - 1 :]]
        tops[slab] = top
        extra[slab] = jnp.concatenate(ends + [jnp.zeros((4, LANES), jnp.float32)], axis=0)
        return 0

    lax.fori_loop(0, slabs, compute, 0, unroll=2)
    ends = extra[...]
    code = scale_code(jnp.max(tops[...], axis=1), FINE)
    factor = encode_factor(code, TOP)
    edge_code = scale_code(jnp.max(jnp.abs(ends), axis=1), 1.0)
    edge_factor = encode_factor(edge_code, EDGE_TOP)
    at_row = lax.broadcasted_iota(jnp.int32, ends.shape, 1)
    ends = jnp.round(ends * edge_factor[:, None, :])
    ends = jnp.where(at_row == 4, edge_code[:, None, :], jnp.where(at_row == 5, code[:, None, :], ends))
    buffer[slabs * rows :, :] = to_int16(ends.reshape(slabs * EXTRA, LANES))
    tops[:, 0, :] = factor

    def code_slab(slab, _):
        buffer[rows_of(slab), :] = to_int16(jnp.round(values[rows_of(slab), :] * tops[slab, 0:1, :]))
        return 0

    lax.fori_loop(0, slabs, code_slab, 0, unroll=2)
    step = pl.program_id(0)
    for at, out in enumerate(outs):

        @pl.when(step == at)
        def _():
            out[...] = buffer[...]


def split_kernel(a_ref, hi_ref, lo_ref):
    a = a_ref[...]
    hi = a.astype(jnp.bfloat16)
    hi_ref[...] = hi
    lo_ref[...] = (a - hi.astype(jnp.float32)).astype(jnp.bfloat16)


def swapped(edges):
    return jnp.concatenate([edges[1:2], edges[0:1], edges[3:4], edges[2:3]], axis=0)


def product_kernel(order, held, first_slab, slabs, lower_slabs, half_cols, where, edge_weight, *refs):
    groups = len(order)
    ins, (hi_ref, lo_ref) = refs[:groups], refs[groups : groups + 2]
    outs, (v_hi, v_lo, y, edges, codes, all_codes) = refs[-6 - groups : -6], refs[-6:]
    size = y.shape[0]
    levels = size // (2 * groups)
    rows = 2 * levels
    me = where[0]
    pair = where[1]
    peers = [lax.bitwise_xor(me, k) for k in order]
    near = lax.broadcasted_iota(jnp.int32, (8, LANES), 0)

    def place(f, peer):
        return pl.ds(pl.multiple_of(f * (size // 2) + peer * levels, levels), levels)

    def one_tile(t, _):
        extras = []
        for ref, peer, (all_slabs, skipped) in zip(ins, peers, held):
            at = all_slabs * rows + (skipped + t * 2) * EXTRA
            two = to_float(ref[pl.ds(pl.multiple_of(at, TILE), TILE), :])
            power = jnp.exp2(two * (1.0 / FINE))
            extras.append(power)
            for j in range(2):
                at = j * EXTRA
                edges[peer, :, j * LANES : (j + 1) * LANES] = two[at : at + 4] * (
                    power[at + 4 : at + 5] * (1.0 / EDGE_TOP)
                )
        for ref, peer, power, (_, skipped) in zip(ins, peers, extras, held):
            before, after = jnp.maximum(peer - 1, 0), jnp.minimum(peer + 1, groups - 1)
            weight_before, weight_after = edge_weight[peer], edge_weight[groups + peer]
            for j in range(2):
                cols = slice(j * LANES, (j + 1) * LANES)
                scale = power[j * EXTRA + 5 : j * EXTRA + 6] * (1.0 / TOP)
                here = swapped(edges[peer, :, cols])
                low = weight_before * (edges[before, :, cols] - here)
                high = weight_after * (edges[after, :, cols] - here)
                start = (skipped + t * 2 + j) * rows
                for f in range(2):
                    v = to_float(ref[pl.ds(pl.multiple_of(start + f * levels, TILE), levels), :]) * scale
                    first = v[:8] + jnp.where(near == 0, low[2 * f + 1 : 2 * f + 2], 0.0)
                    last = v[levels - 8 :] + jnp.where(near == 7, high[2 * f : 2 * f + 1], 0.0)
                    middle = [v[8 : levels - 8]] if levels > 16 else []
                    v = jnp.concatenate([first] + middle + [last], axis=0)
                    hi = v.astype(jnp.bfloat16)
                    v_hi[place(f, peer), cols] = hi
                    v_lo[place(f, peer), cols] = (v - hi.astype(jnp.float32)).astype(jnp.bfloat16)

        def product(which, cols):
            dot = functools.partial(jnp.dot, preferred_element_type=jnp.float32)
            return (
                dot(lo_ref[which], v_hi[:, cols])
                + dot(hi_ref[which], v_lo[:, cols])
                + dot(hi_ref[which], v_hi[:, cols])
            )

        y[...] = product(1, slice(0, 2 * LANES))
        for tile in range(slabs // 2):
            for j in range(2):
                first_col = (first_slab + tile * 2 + j) * LANES
                if first_col % half_cols < lower_slabs * LANES:

                    @pl.when(t == tile)
                    def _():
                        cols = slice(j * LANES, (j + 1) * LANES)
                        column = first_col % half_cols + lax.broadcasted_iota(jnp.int32, (size, LANES), 1)
                        bound = pair + 1 if first_col < half_cols else pair
                        y[:, cols] = jnp.where(column < bound, product(0, cols), y[:, cols])

        def results(peer, j):
            return jnp.concatenate([y[place(f, peer), j * LANES : (j + 1) * LANES] for f in range(2)], axis=0)

        for i, peer in enumerate(peers):
            for j in range(2):
                v = jnp.abs(results(peer, j))
                codes[j, i] = jnp.max(v.reshape(rows // 8, 8, LANES), axis=0)
        code = scale_code(jnp.max(codes[...], axis=2), FINE)
        factor = encode_factor(code, TOP)
        for i, (out, peer) in enumerate(zip(outs, peers)):
            for j in range(2):
                start = (t * 2 + j) * rows
                out[pl.ds(pl.multiple_of(start, TILE), rows), :] = to_int16(
                    jnp.round(results(peer, j) * factor[j, i : i + 1])
                )
                all_codes[i, pl.ds(t * 2 + j, 1), :] = code[j, i : i + 1]
        return 0

    all_codes[...] = jnp.zeros_like(all_codes)
    lax.fori_loop(0, slabs // 2, one_tile, 0)
    for i, out in enumerate(outs):
        out[slabs * rows :, :] = to_int16(all_codes[i])


def result_kernel(count, slabs, where, *refs):
    ins, out_ref, buffer = refs[:count], refs[-2], refs[-1]
    levels = out_ref.shape[1]
    rows = 2 * levels
    step = pl.program_id(0)
    for at in range(count):

        @pl.when(step == at)
        def _():
            buffer[...] = ins[at][...]

    scales = scale_of(to_float(buffer[slabs * rows :, :]), TOP)
    for slab in range(slabs):
        for f in range(2):
            start = slab * rows + f * levels
            v = to_float(buffer[start : start + levels, :])
            out_ref[f, :, slab * LANES : (slab + 1) * LANES] = v * scales[slab : slab + 1, :]


def send(message, k, groups):
    return message if k == 0 else lax.ppermute(message, "rad", [(i, i ^ k) for i in range(groups)])


def columns_of(ks, width, first):
    def at(step, w):
        k = jnp.int32(ks[-1])
        for i, value in enumerate(ks[:-1]):
            k = jnp.where(step == i, value, k)
        return (0, 0, pl.multiple_of(lax.bitwise_xor(w[0], k) * width + first, LANES))

    return at


def columns_block(levels, count, index_map):
    return pl.BlockSpec((pl.Element(2), pl.Element(levels), pl.Element(count)), index_map)


def local(slots, nonlin, state, inverse, pair_of_slot):
    levels = nonlin.shape[1]
    groups = lax.axis_size("rad")
    width = nonlin.shape[2] // groups
    size = inverse.shape[-1]
    all_slabs = width // LANES
    shares = [(first * all_slabs // 8, count * all_slabs // 8) for first, count in SHARES]
    rows = 2 * levels
    lower_slabs = -(-slots // LANES)
    me = lax.axis_index("rad").astype(jnp.int32)
    where = jnp.stack([me, pair_of_slot[0].astype(jnp.int32)])
    weights = stencil_table(levels * groups)
    table = jnp.asarray(weights)
    edge_weight = jnp.asarray(np.concatenate([weights[::levels, 0], weights[levels - 1 :: levels, 2]]))
    vmem = pl.BlockSpec(memory_space=pltpu.VMEM)
    hbm = pl.BlockSpec(memory_space=pl.ANY)
    far = list(range(groups // 2, groups))
    near = list(range(groups // 2))
    others = near[1:]
    order = []
    for i, k in enumerate(far):
        order += [k] + others[2 * i : 2 * i + 2]
    order += near[:1]

    def call(kernel, name, flops, moved, vmem_mib, **kwargs):
        return pl.pallas_call(
            kernel,
            name=name,
            compiler_params=pltpu.CompilerParams(vmem_limit_bytes=vmem_mib * MIB),
            cost_estimate=pl.CostEstimate(flops=flops, bytes_accessed=moved, transcendentals=0),
            **kwargs,
        )

    def right_side(ks, cut, *earlier):
        first, held = cut
        block = columns_block(levels, held * LANES, columns_of(ks, width, first * LANES))
        out_rows = held * (rows + EXTRA)
        return call(
            functools.partial(right_side_kernel, held, len(ks)),
            "right_side",
            MIB * len(ks),
            MIB * len(ks),
            56,
            out_shape=[jax.ShapeDtypeStruct((out_rows, LANES), jnp.int16)] * len(ks),
            grid_spec=pltpu.PrefetchScalarGridSpec(
                num_scalar_prefetch=1,
                grid=(len(ks),),
                in_specs=[block, block, pl.BlockSpec((levels, LANES), lambda k, w: (w[0], 0)), *[hbm for _ in earlier]],
                out_specs=[pl.BlockSpec((out_rows, LANES), lambda k, w: (0, 0))] * len(ks),
                scratch_shapes=[
                    pltpu.VMEM((out_rows, LANES), jnp.int16),
                    pltpu.VMEM((held * rows, LANES), jnp.float32),
                    pltpu.VMEM((held, 8, LANES), jnp.float32),
                    pltpu.VMEM((held, EXTRA, LANES), jnp.float32),
                ],
            ),
        )(where, nonlin, state, table, *earlier)

    def split():
        block = pl.BlockSpec((1, size // 4, size), lambda i, j: (i, j, 0))
        half = jax.ShapeDtypeStruct((2, size, size), jnp.bfloat16)
        return call(
            split_kernel,
            "split_inverse",
            4 * MIB,
            16 * MIB,
            16,
            out_shape=[half, half],
            grid=(2, 4),
            in_specs=[block],
            out_specs=[block, block],
        )(inverse[0])

    def product(cut, messages, held, hi, lo, *earlier):
        first, slabs = cut
        return call(
            functools.partial(product_kernel, order, held, first, slabs, lower_slabs, width // 2),
            "product",
            6 * size * size * slabs * LANES,
            10 * MIB,
            32,
            out_shape=[jax.ShapeDtypeStruct((slabs * rows + TILE, LANES), jnp.int16)] * groups,
            grid_spec=pltpu.PrefetchScalarGridSpec(
                num_scalar_prefetch=1,
                grid=(),
                in_specs=[pl.BlockSpec(memory_space=pltpu.SMEM)]
                + [vmem] * (groups + 2)
                + [hbm for _ in earlier],
                out_specs=[vmem] * groups,
                scratch_shapes=[
                    pltpu.VMEM((size, 2 * LANES), jnp.bfloat16),
                    pltpu.VMEM((size, 2 * LANES), jnp.bfloat16),
                    pltpu.VMEM((size, 2 * LANES), jnp.float32),
                    pltpu.VMEM((groups, 4, 2 * LANES), jnp.float32),
                    pltpu.VMEM((2, groups, 8, LANES), jnp.float32),
                    pltpu.VMEM((groups, TILE, LANES), jnp.float32),
                ],
            ),
        )(where, edge_weight, *messages, hi, lo, *earlier)

    def result(ks, cut, messages, previous):
        first, slabs = cut
        carried = [] if previous is None else [previous]
        return call(
            functools.partial(result_kernel, len(ks), slabs),
            "result",
            MIB,
            2 * MIB,
            16,
            out_shape=jax.ShapeDtypeStruct(state.shape, jnp.float32),
            grid_spec=pltpu.PrefetchScalarGridSpec(
                num_scalar_prefetch=1,
                grid=(len(ks),),
                in_specs=[pl.BlockSpec(m.shape, lambda k, w: (0, 0)) for m in messages] + [hbm] * len(carried),
                out_specs=columns_block(levels, slabs * LANES, columns_of(ks, width, first * LANES)),
                scratch_shapes=[pltpu.VMEM(messages[0].shape, jnp.int16)],
            ),
            input_output_aliases={} if previous is None else {len(ks) + 1: 0},
        )(where, *messages, *carried)

    made, got = [], {}
    for ks, cut in ((far[:2], shares[0]), (near, shares[0]), (far[2:], shares[0]), (far, shares[1]), (near, shares[1])):
        made = right_side(ks, cut, *made[-1:])
        got.update({(k, cut): send(m, k, groups) for k, m in zip(ks, made)})
    hi, lo = split()
    back, made = [], []
    for first, count in shares:
        messages, held = [], []
        for k in order:
            cut = next(c for j, c in got if j == k and c[0] <= first < sum(c))
            messages.append(got[k, cut])
            held.append((cut[1], first - cut[0]))
        made = product((first, count), messages, tuple(held), hi, lo, *made[-1:])
        back.append({k: send(m, k, groups) for k, m in zip(order, made)})
    out = None
    for i, (cut, came) in enumerate(zip(shares, back)):
        for ks in [order] if i < len(shares) - 1 else [order[:4] + order[-1:], order[4:-1]]:
            out = result(ks, cut, [came[k] for k in ks], out)
    return out


def solution(mesh):
    placed = (
        P(None, "rad", "ang"),
        P(None, "rad", "ang"),
        P(("ang", "rad"), None, None, None),
        P(("ang", "rad")),
    )
    slots = mesh.shape["rad"] * mesh.shape["ang"]
    return jax.shard_map(
        functools.partial(local, slots),
        mesh=mesh,
        in_specs=placed,
        out_specs=P(None, "rad", "ang"),
        check_vma=False,
    )
```

```python
import functools
import math

import jax
import jax.numpy as jnp
import numpy as np
from jax import lax
from jax.experimental import pallas as pl
from jax.experimental.pallas import tpu as pltpu
from jax.sharding import PartitionSpec as P

inner_radius = 0.35
outer_radius = 1.0
blend_weight = 0.5

LANES = 128
TILE = 16
EXTRA = 8
CHUNKS = 2
TOP = 32700.0
EDGE_TOP = 16384.0
FINE = 128.0
MIB = 1024 * 1024


def radius_at(level_index, total_levels):
    scaled = level_index / (total_levels - 1.0)
    stretch = (1.0 - blend_weight) * scaled + blend_weight * (1.0 - np.cos(math.pi * scaled)) / 2.0
    return inner_radius + (outer_radius - inner_radius) * stretch


def stencil_table(total_levels):
    k = np.arange(total_levels, dtype=np.float64)
    radius = radius_at(k, total_levels)
    below = radius - radius_at(k - 1.0, total_levels)
    above = radius_at(k + 1.0, total_levels) - radius
    at_inner, at_outer = k == 0, k == total_levels - 1
    weight_below = np.where(at_inner, 0.0, np.where(at_outer, -1.0 / below, -above / (below * (below + above))))
    weight_here = np.where(
        at_inner, -1.0 / above, np.where(at_outer, 1.0 / below, (above - below) / (below * above))
    )
    weight_above = np.where(at_inner, 1.0 / above, np.where(at_outer, 0.0, below / (above * (below + above))))
    time_step = 0.5 * (outer_radius - inner_radius) / (total_levels - 1.0)
    table = np.zeros((total_levels, LANES), np.float32)
    table[:, 0] = time_step * weight_below
    table[:, 1] = time_step * (weight_here + 2.0 / radius)
    table[:, 2] = time_step * weight_above
    return table


def scale_code(largest, per_octave):
    return jnp.ceil(jnp.log2(jnp.maximum(largest, 1e-30)) * per_octave) * (FINE / per_octave)


def encode_factor(code, top):
    return jnp.exp2(code * (-1.0 / FINE)) * top


def to_int16(values):
    return values.astype(jnp.int32).astype(jnp.int16)


def to_float(codes):
    return codes.astype(jnp.int32).astype(jnp.float32)


def scale_of(codes, top):
    return jnp.exp2(codes * (1.0 / FINE)) * (1.0 / top)


def lanes_of(slab):
    return pl.ds(pl.multiple_of(slab * LANES, LANES), LANES)


def right_side_kernel(slabs, partners, where, n_low, n_high, s_low, s_high, tab_ref, *refs):
    outs, (buffer, values, tops, extra) = refs[-4 - partners : -4], refs[-4:]
    levels = n_low.shape[1]
    rows = 2 * levels
    tab = tab_ref[...]
    below, here, above = (jnp.broadcast_to(tab[:, i : i + 1], (levels, LANES)) for i in range(3))
    row = lax.broadcasted_iota(jnp.int32, (levels, LANES), 0)

    def rows_of(slab):
        return pl.ds(pl.multiple_of(slab * rows, rows), rows)

    def compute(pair, _):
        cols = lanes_of(pair)
        for half, (n_ref, s_ref) in enumerate(((n_low, s_low), (n_high, s_high))):
            slab = pair * 2 + half
            ends, top = [], jnp.zeros((8, LANES), jnp.float32)
            for f in range(2):
                n = n_ref[f, :, cols].astype(jnp.float32)
                prev = jnp.where(row == 0, n, pltpu.roll(n, 1, 0))
                succ = jnp.where(row == levels - 1, n, pltpu.roll(n, levels - 1, 0))
                v = s_ref[f, :, cols] + (below * prev + here * n + above * succ)
                values[pl.ds(pl.multiple_of(slab * rows + f * levels, levels), levels), :] = v
                top = jnp.maximum(top, jnp.max(jnp.abs(v).reshape(levels // 8, 8, LANES), axis=0))
                ends += [n[:1], n[levels - 1 :]]
            tops[slab] = top
            extra[slab] = jnp.concatenate(ends + [jnp.zeros((4, LANES), jnp.float32)], axis=0)
        return 0

    lax.fori_loop(0, slabs // 2, compute, 0)
    ends = extra[...]
    code = scale_code(jnp.max(tops[...], axis=1), FINE)
    factor = encode_factor(code, TOP)
    edge_code = scale_code(jnp.max(jnp.abs(ends), axis=1), 1.0)
    edge_factor = encode_factor(edge_code, EDGE_TOP)
    at_row = lax.broadcasted_iota(jnp.int32, ends.shape, 1)
    ends = jnp.round(ends * edge_factor[:, None, :])
    ends = jnp.where(at_row == 4, edge_code[:, None, :], jnp.where(at_row == 5, code[:, None, :], ends))
    buffer[slabs * rows :, :] = to_int16(ends.reshape(slabs * EXTRA, LANES))
    tops[:, 0, :] = factor

    def code_slab(slab, _):
        buffer[rows_of(slab), :] = to_int16(jnp.round(values[rows_of(slab), :] * tops[slab, 0:1, :]))
        return 0

    lax.fori_loop(0, slabs, code_slab, 0, unroll=2)
    step = pl.program_id(0)
    for at, out in enumerate(outs):

        @pl.when(step == at)
        def _():
            out[...] = buffer[...]


def split_kernel(a_ref, both_ref):
    a = a_ref[...]
    size = a.shape[-1]
    hi = a.astype(jnp.bfloat16)
    both_ref[:, :, size:] = hi
    both_ref[:, :, :size] = (a - hi.astype(jnp.float32)).astype(jnp.bfloat16)


def swapped(edges):
    return jnp.concatenate([edges[1:2], edges[0:1], edges[3:4], edges[2:3]], axis=0)


def product_kernel(order, first_slab, slabs, lower_slabs, where, edge_weight, *refs):
    groups = len(order)
    ins, both_ref = refs[:groups], refs[groups]
    outs, scratch, all_codes = refs[-groups - 9 : -9], refs[-9:-1], refs[-1]
    size = both_ref.shape[1]
    levels = size // (2 * groups)
    rows = 2 * levels
    me = where[0]
    pair = where[1]
    peers = [lax.bitwise_xor(me, k) for k in order]
    near = lax.broadcasted_iota(jnp.int32, (8, LANES), 0)

    def place(f, peer):
        return pl.ds(pl.multiple_of(f * (size // 2) + peer * levels, levels), levels)

    def one_tile(t):
        v_both, y, edges, codes = scratch[t % 2 * 4 : t % 2 * 4 + 4]
        extras = []
        for ref, peer in zip(ins, peers):
            at = slabs * rows + t * TILE
            two = to_float(ref[at : at + TILE, :])
            power = jnp.exp2(two * (1.0 / FINE))
            extras.append(power)
            for j in range(2):
                at = j * EXTRA
                edges[peer, :, j * LANES : (j + 1) * LANES] = two[at : at + 4] * (
                    power[at + 4 : at + 5] * (1.0 / EDGE_TOP)
                )
        for ref, peer, power in zip(ins, peers, extras):
            before, after = jnp.maximum(peer - 1, 0), jnp.minimum(peer + 1, groups - 1)
            weight_before, weight_after = edge_weight[peer], edge_weight[groups + peer]
            for j in range(2):
                cols = slice(j * LANES, (j + 1) * LANES)
                scale = power[j * EXTRA + 5 : j * EXTRA + 6] * (1.0 / TOP)
                here = swapped(edges[peer, :, cols])
                low = weight_before * (edges[before, :, cols] - here)
                high = weight_after * (edges[after, :, cols] - here)
                start = (t * 2 + j) * rows
                for f in range(2):
                    v = to_float(ref[start + f * levels : start + (f + 1) * levels, :]) * scale
                    first = v[:8] + jnp.where(near == 0, low[2 * f + 1 : 2 * f + 2], 0.0)
                    last = v[levels - 8 :] + jnp.where(near == 7, high[2 * f : 2 * f + 1], 0.0)
                    middle = [v[8 : levels - 8]] if levels > 16 else []
                    v = jnp.concatenate([first] + middle + [last], axis=0)
                    hi = v.astype(jnp.bfloat16)
                    v_both[place(f, peer), cols] = hi
                    v_both[place(f + 2, peer), cols] = (v - hi.astype(jnp.float32)).astype(jnp.bfloat16)

        def product(which):
            dot = functools.partial(jnp.dot, preferred_element_type=jnp.float32)
            return dot(both_ref[which], v_both[...]) + dot(both_ref[which, :, size:], v_both[:size, :])

        upper = product(1)
        if first_slab + t < lower_slabs:
            lane = lax.broadcasted_iota(jnp.int32, upper.shape, 1)
            column = (first_slab + t) * LANES + jnp.where(lane < LANES, lane, lane - LANES + 1)
            y[...] = jnp.where(column < pair + 1, product(0), upper)
        else:
            y[...] = upper

        def results(peer, j):
            return jnp.concatenate([y[place(f, peer), j * LANES : (j + 1) * LANES] for f in range(2)], axis=0)

        for i, peer in enumerate(peers):
            for j in range(2):
                v = jnp.abs(results(peer, j))
                codes[j, i] = jnp.max(v.reshape(rows // 8, 8, LANES), axis=0)
        code = scale_code(jnp.max(codes[...], axis=2), FINE)
        factor = encode_factor(code, TOP)
        for i, (out, peer) in enumerate(zip(outs, peers)):
            for j in range(2):
                start = (t * 2 + j) * rows
                out[start : start + rows, :] = to_int16(
                    jnp.round(results(peer, j) * factor[j, i : i + 1])
                )
                all_codes[i, t * 2 + j : t * 2 + j + 1, :] = code[j, i : i + 1]

    all_codes[...] = jnp.zeros_like(all_codes)
    for t in range(slabs // 2):
        one_tile(t)
    for i, out in enumerate(outs):
        out[slabs * rows :, :] = to_int16(all_codes[i])


def result_kernel(ks, slabs, skipped, width, where, *refs):
    count = len(ks)
    ins, (out_ref, buffer, sems) = refs[:count], refs[-3:]
    levels = out_ref.shape[1]
    rows = 2 * levels
    span = slabs // 2 * LANES
    copies = []
    for at, (message, k) in enumerate(zip(ins, ks)):
        scales = scale_of(to_float(message[slabs * rows :, :]), TOP)
        first_col = lax.bitwise_xor(where[0], k) * width + skipped
        for half in range(2):
            for pair in range(slabs // 2):
                slab = pair * 2 + half
                for f in range(2):
                    start = slab * rows + f * levels
                    v = to_float(message[start : start + levels, :])
                    buffer[at, half, f, :, pair * LANES : (pair + 1) * LANES] = v * scales[slab : slab + 1, :]
            cols = pl.ds(pl.multiple_of(first_col + half * (width // 2), LANES), span)
            copies.append(pltpu.make_async_copy(buffer.at[at, half], out_ref.at[:, :, cols], sems.at[at, half]))
            copies[-1].start()
    for copy in copies:
        copy.wait()


def send(message, k, groups):
    return message if k == 0 else lax.ppermute(message, "rad", [(i, i ^ k) for i in range(groups)])


def columns_of(ks, width, first):
    def at(step, w):
        k = jnp.int32(ks[-1])
        for i, value in enumerate(ks[:-1]):
            k = jnp.where(step == i, value, k)
        return (0, 0, pl.multiple_of(lax.bitwise_xor(w[0], k) * width + first, LANES))

    return at


def columns_block(levels, count, index_map):
    return pl.BlockSpec((pl.Element(2), pl.Element(levels), pl.Element(count)), index_map)


def local(slots, nonlin, state, inverse, pair_of_slot):
    levels = nonlin.shape[1]
    groups = lax.axis_size("rad")
    width = nonlin.shape[2] // groups
    size = inverse.shape[-1]
    all_slabs = width // LANES
    half_cols = width // 2
    span = half_cols // CHUNKS
    slabs = 2 * span // LANES
    rows = 2 * levels
    lower_slabs = -(-slots // LANES)
    me = lax.axis_index("rad").astype(jnp.int32)
    where = jnp.stack([me, pair_of_slot[0].astype(jnp.int32)])
    weights = stencil_table(levels * groups)
    table = jnp.asarray(weights)
    edge_weight = jnp.asarray(np.concatenate([weights[::levels, 0], weights[levels - 1 :: levels, 2]]))
    vmem = pl.BlockSpec(memory_space=pltpu.VMEM)
    hbm = pl.BlockSpec(memory_space=pl.ANY)
    far = list(range(groups // 2, groups))
    near = list(range(groups // 2))
    others = near[1:]
    order = []
    for i, k in enumerate(far):
        order += [k] + others[2 * i : 2 * i + 2]
    order += near[:1]

    def call(kernel, name, flops, moved, vmem_mib, **kwargs):
        return pl.pallas_call(
            kernel,
            name=name,
            compiler_params=pltpu.CompilerParams(vmem_limit_bytes=vmem_mib * MIB),
            cost_estimate=pl.CostEstimate(flops=flops, bytes_accessed=moved, transcendentals=0),
            **kwargs,
        )

    def right_side(ks, chunk, *earlier):
        low, high = (
            columns_block(levels, span, columns_of(ks, width, first))
            for first in (chunk * span, half_cols + chunk * span)
        )
        out_rows = slabs * (rows + EXTRA)
        return call(
            functools.partial(right_side_kernel, slabs, len(ks)),
            "right_side",
            MIB * len(ks),
            MIB * len(ks),
            56,
            out_shape=[jax.ShapeDtypeStruct((out_rows, LANES), jnp.int16)] * len(ks),
            grid_spec=pltpu.PrefetchScalarGridSpec(
                num_scalar_prefetch=1,
                grid=(len(ks),),
                in_specs=[low, high, low, high, pl.BlockSpec((levels, LANES), lambda k, w: (w[0], 0))]
                + [hbm for _ in earlier],
                out_specs=[pl.BlockSpec((out_rows, LANES), lambda k, w: (0, 0))] * len(ks),
                scratch_shapes=[
                    pltpu.VMEM((out_rows, LANES), jnp.int16),
                    pltpu.VMEM((slabs * rows, LANES), jnp.float32),
                    pltpu.VMEM((slabs, 8, LANES), jnp.float32),
                    pltpu.VMEM((slabs, EXTRA, LANES), jnp.float32),
                ],
            ),
        )(where, nonlin, nonlin, state, state, table, *earlier)

    def split():
        block = pl.BlockSpec((1, size // 4, size), lambda i, j: (i, j, 0))
        return call(
            split_kernel,
            "split_inverse",
            4 * MIB,
            16 * MIB,
            16,
            out_shape=jax.ShapeDtypeStruct((2, size, 2 * size), jnp.bfloat16),
            grid=(2, 4),
            in_specs=[block],
            out_specs=pl.BlockSpec((1, size // 4, 2 * size), lambda i, j: (i, j, 0)),
        )(inverse[0])

    def product(chunk, messages, both, *earlier):
        return call(
            functools.partial(product_kernel, order, chunk * span // LANES, slabs, lower_slabs),
            "product",
            6 * size * size * slabs * LANES,
            10 * MIB,
            32,
            out_shape=[jax.ShapeDtypeStruct((slabs * rows + TILE, LANES), jnp.int16)] * groups,
            grid_spec=pltpu.PrefetchScalarGridSpec(
                num_scalar_prefetch=1,
                grid=(),
                in_specs=[pl.BlockSpec(memory_space=pltpu.SMEM)]
                + [vmem] * (groups + 1)
                + [hbm for _ in earlier],
                out_specs=[vmem] * groups,
                scratch_shapes=2
                * [
                    pltpu.VMEM((2 * size, 2 * LANES), jnp.bfloat16),
                    pltpu.VMEM((size, 2 * LANES), jnp.float32),
                    pltpu.VMEM((groups, 4, 2 * LANES), jnp.float32),
                    pltpu.VMEM((2, groups, 8, LANES), jnp.float32),
                ]
                + [pltpu.VMEM((groups, TILE, LANES), jnp.float32)],
            ),
        )(where, edge_weight, *messages, both, *earlier)

    def result(ks, chunk, messages, previous):
        carried = [] if previous is None else [previous]
        return call(
            functools.partial(result_kernel, ks, slabs, chunk * span, width),
            "result",
            MIB,
            2 * MIB,
            16,
            out_shape=jax.ShapeDtypeStruct(state.shape, jnp.float32),
            grid_spec=pltpu.PrefetchScalarGridSpec(
                num_scalar_prefetch=1,
                grid=(),
                in_specs=[vmem] * len(messages) + [hbm] * len(carried),
                out_specs=hbm,
                scratch_shapes=[
                    pltpu.VMEM((len(ks), 2, 2, levels, span), jnp.float32),
                    pltpu.SemaphoreType.DMA((len(ks), 2)),
                ],
            ),
            input_output_aliases={} if previous is None else {len(ks) + 1: 0},
        )(where, *messages, *carried)

    made, got = [], {}
    for ks, chunk in ((far[:2], 0), (near + far[2:], 0), (far + near, 1)):
        made = right_side(ks, chunk, *made[-1:])
        got.update({(k, chunk): send(m, k, groups) for k, m in zip(ks, made)})
    both = split()
    back, made = [], []
    for chunk in range(CHUNKS):
        made = product(chunk, [got[k, chunk] for k in order], both, *made[-1:])
        back.append({k: send(m, k, groups) for k, m in zip(order, made)})
    out = None
    for chunk, came in enumerate(back):
        for ks in [order] if chunk < CHUNKS - 1 else [order[:4] + order[-1:], order[4:-1]]:
            out = result(ks, chunk, [came[k] for k in ks], out)
    return out


def solution(mesh):
    placed = (
        P(None, "rad", "ang"),
        P(None, "rad", "ang"),
        P(("ang", "rad"), None, None, None),
        P(("ang", "rad")),
    )
    slots = mesh.shape["rad"] * mesh.shape["ang"]
    return jax.shard_map(
        functools.partial(local, slots),
        mesh=mesh,
        in_specs=placed,
        out_specs=P(None, "rad", "ang"),
        check_vma=False,
    )
```

```python
import functools
import math

import jax
import jax.numpy as jnp
import numpy as np
from jax import lax
from jax.experimental import pallas as pl
from jax.experimental.pallas import tpu as pltpu
from jax.sharding import PartitionSpec as P

inner_radius = 0.35
outer_radius = 1.0
blend_weight = 0.5

LANES = 128
TILE = 16
EXTRA = 8
CHUNKS = 2
TOP = 32700.0
EDGE_TOP = 16384.0
FINE = 128.0
MIB = 1024 * 1024


def radius_at(level_index, total_levels):
    scaled = level_index / (total_levels - 1.0)
    stretch = (1.0 - blend_weight) * scaled + blend_weight * (1.0 - np.cos(math.pi * scaled)) / 2.0
    return inner_radius + (outer_radius - inner_radius) * stretch


def stencil_table(total_levels):
    k = np.arange(total_levels, dtype=np.float64)
    radius = radius_at(k, total_levels)
    below = radius - radius_at(k - 1.0, total_levels)
    above = radius_at(k + 1.0, total_levels) - radius
    at_inner, at_outer = k == 0, k == total_levels - 1
    weight_below = np.where(at_inner, 0.0, np.where(at_outer, -1.0 / below, -above / (below * (below + above))))
    weight_here = np.where(
        at_inner, -1.0 / above, np.where(at_outer, 1.0 / below, (above - below) / (below * above))
    )
    weight_above = np.where(at_inner, 1.0 / above, np.where(at_outer, 0.0, below / (above * (below + above))))
    time_step = 0.5 * (outer_radius - inner_radius) / (total_levels - 1.0)
    table = np.zeros((total_levels, LANES), np.float32)
    table[:, 0] = time_step * weight_below
    table[:, 1] = time_step * (weight_here + 2.0 / radius)
    table[:, 2] = time_step * weight_above
    return table


def scale_code(largest, per_octave):
    return jnp.ceil(jnp.log2(jnp.maximum(largest, 1e-30)) * per_octave) * (FINE / per_octave)


def encode_factor(code, top):
    return jnp.exp2(code * (-1.0 / FINE)) * top


def to_int16(values):
    return values.astype(jnp.int32).astype(jnp.int16)


def to_float(codes):
    return codes.astype(jnp.int32).astype(jnp.float32)


def scale_of(codes, top):
    return jnp.exp2(codes * (1.0 / FINE)) * (1.0 / top)


def lanes_of(slab):
    return pl.ds(pl.multiple_of(slab * LANES, LANES), LANES)


def right_side_kernel(ks, slabs, skipped, width, nonlin, state, table, *refs):
    count = len(ks)
    outs, (n_buf, s_buf, tab_buf, messages, values, tops, extra, sems, out_sems) = refs[-9 - count : -9], refs[-9:]
    levels = nonlin.shape[1]
    rows = 2 * levels
    span = slabs // 2 * LANES
    me = lax.axis_index("rad")

    def fetches(at, first):
        made = []
        for half in range(2):
            cols = pl.ds(pl.multiple_of(first + half * (width // 2), LANES), span)
            made.append(pltpu.make_async_copy(nonlin.at[:, :, cols], n_buf.at[at, half], sems.at[at, half, 0]))
            made.append(pltpu.make_async_copy(state.at[:, :, cols], s_buf.at[at, half], sems.at[at, half, 1]))
        return made

    here_rows = pl.ds(pl.multiple_of(me * levels, levels), levels)
    tab_copy = pltpu.make_async_copy(table.at[here_rows, :], tab_buf, out_sems.at[count])
    tab_copy.start()
    for at, k in enumerate(ks):
        for copy in fetches(at, lax.bitwise_xor(me, k) * width + skipped):
            copy.start()
    tab_copy.wait()
    tab = tab_buf[...]
    below, here, above = (jnp.broadcast_to(tab[:, i : i + 1], (levels, LANES)) for i in range(3))
    row = lax.broadcasted_iota(jnp.int32, (levels, LANES), 0)

    def rows_of(slab):
        return pl.ds(pl.multiple_of(slab * rows, rows), rows)

    def one_partner(at, _):
        for copy in fetches(at, 0):
            copy.wait()

        def compute(pair, _):
            cols = lanes_of(pair)
            for half in range(2):
                slab = pair * 2 + half
                ends, top = [], jnp.zeros((8, LANES), jnp.float32)
                for f in range(2):
                    n = n_buf[at, half, f, :, cols].astype(jnp.float32)
                    prev = jnp.where(row == 0, n, pltpu.roll(n, 1, 0))
                    succ = jnp.where(row == levels - 1, n, pltpu.roll(n, levels - 1, 0))
                    v = s_buf[at, half, f, :, cols] + (below * prev + here * n + above * succ)
                    values[pl.ds(pl.multiple_of(slab * rows + f * levels, levels), levels), :] = v
                    top = jnp.maximum(top, jnp.max(jnp.abs(v).reshape(levels // 8, 8, LANES), axis=0))
                    ends += [n[:1], n[levels - 1 :]]
                tops[slab] = top
                extra[slab] = jnp.concatenate(ends + [jnp.zeros((4, LANES), jnp.float32)], axis=0)
            return 0

        lax.fori_loop(0, slabs // 2, compute, 0)
        ends = extra[...]
        code = scale_code(jnp.max(tops[...], axis=1), FINE)
        factor = encode_factor(code, TOP)
        edge_code = scale_code(jnp.max(jnp.abs(ends), axis=1), 1.0)
        edge_factor = encode_factor(edge_code, EDGE_TOP)
        at_row = lax.broadcasted_iota(jnp.int32, ends.shape, 1)
        ends = jnp.round(ends * edge_factor[:, None, :])
        ends = jnp.where(at_row == 4, edge_code[:, None, :], jnp.where(at_row == 5, code[:, None, :], ends))
        messages[at, slabs * rows :, :] = to_int16(ends.reshape(slabs * EXTRA, LANES))
        tops[:, 0, :] = factor

        def code_slab(slab, _):
            messages[at, rows_of(slab), :] = to_int16(jnp.round(values[rows_of(slab), :] * tops[slab, 0:1, :]))
            return 0

        lax.fori_loop(0, slabs, code_slab, 0, unroll=2)
        for i, out in enumerate(outs):

            @pl.when(at == i)
            def _():
                pltpu.make_async_copy(messages.at[i], out, out_sems.at[i]).start()

        return 0

    lax.fori_loop(0, count, one_partner, 0)
    for i, out in enumerate(outs):
        pltpu.make_async_copy(messages.at[i], out, out_sems.at[i]).wait()


def split_kernel(a_ref, both_ref):
    a = a_ref[...]
    size = a.shape[-1]
    hi = a.astype(jnp.bfloat16)
    both_ref[:, :, size:] = hi
    both_ref[:, :, :size] = (a - hi.astype(jnp.float32)).astype(jnp.bfloat16)


def swapped(edges):
    return jnp.concatenate([edges[1:2], edges[0:1], edges[3:4], edges[2:3]], axis=0)


def product_kernel(order, first_slab, slabs, lower_slabs, pair_ref, edge_weight, *refs):
    groups = len(order)
    ins, both_ref = refs[:groups], refs[groups]
    outs, scratch, all_codes = refs[-groups - 9 : -9], refs[-9:-1], refs[-1]
    size = both_ref.shape[1]
    levels = size // (2 * groups)
    rows = 2 * levels
    me = lax.axis_index("rad")
    pair = pair_ref[0]
    peers = [lax.bitwise_xor(me, k) for k in order]
    near = lax.broadcasted_iota(jnp.int32, (8, LANES), 0)

    def place(f, peer):
        return pl.ds(pl.multiple_of(f * (size // 2) + peer * levels, levels), levels)

    def one_tile(t):
        v_both, y, edges, codes = scratch[t % 2 * 4 : t % 2 * 4 + 4]
        extras = []
        for ref, peer in zip(ins, peers):
            at = slabs * rows + t * TILE
            two = to_float(ref[at : at + TILE, :])
            power = jnp.exp2(two * (1.0 / FINE))
            extras.append(power)
            for j in range(2):
                at = j * EXTRA
                edges[peer, :, j * LANES : (j + 1) * LANES] = two[at : at + 4] * (
                    power[at + 4 : at + 5] * (1.0 / EDGE_TOP)
                )
        for ref, peer, power in zip(ins, peers, extras):
            before, after = jnp.maximum(peer - 1, 0), jnp.minimum(peer + 1, groups - 1)
            weight_before, weight_after = edge_weight[peer], edge_weight[groups + peer]
            for j in range(2):
                cols = slice(j * LANES, (j + 1) * LANES)
                scale = power[j * EXTRA + 5 : j * EXTRA + 6] * (1.0 / TOP)
                here = swapped(edges[peer, :, cols])
                low = weight_before * (edges[before, :, cols] - here)
                high = weight_after * (edges[after, :, cols] - here)
                start = (t * 2 + j) * rows
                for f in range(2):
                    v = to_float(ref[start + f * levels : start + (f + 1) * levels, :]) * scale
                    first = v[:8] + jnp.where(near == 0, low[2 * f + 1 : 2 * f + 2], 0.0)
                    last = v[levels - 8 :] + jnp.where(near == 7, high[2 * f : 2 * f + 1], 0.0)
                    middle = [v[8 : levels - 8]] if levels > 16 else []
                    v = jnp.concatenate([first] + middle + [last], axis=0)
                    hi = v.astype(jnp.bfloat16)
                    v_both[place(f, peer), cols] = hi
                    v_both[place(f + 2, peer), cols] = (v - hi.astype(jnp.float32)).astype(jnp.bfloat16)

        def product(which):
            dot = functools.partial(jnp.dot, preferred_element_type=jnp.float32)
            return dot(both_ref[which], v_both[...]) + dot(both_ref[which, :, size:], v_both[:size, :])

        upper = product(1)
        if first_slab + t < lower_slabs:
            lane = lax.broadcasted_iota(jnp.int32, upper.shape, 1)
            column = (first_slab + t) * LANES + jnp.where(lane < LANES, lane, lane - LANES + 1)
            y[...] = jnp.where(column < pair + 1, product(0), upper)
        else:
            y[...] = upper

        def results(peer, j):
            return jnp.concatenate([y[place(f, peer), j * LANES : (j + 1) * LANES] for f in range(2)], axis=0)

        for i, peer in enumerate(peers):
            for j in range(2):
                v = jnp.abs(results(peer, j))
                codes[j, i] = jnp.max(v.reshape(rows // 8, 8, LANES), axis=0)
        code = scale_code(jnp.max(codes[...], axis=2), FINE)
        factor = encode_factor(code, TOP)
        for i, (out, peer) in enumerate(zip(outs, peers)):
            for j in range(2):
                start = (t * 2 + j) * rows
                out[start : start + rows, :] = to_int16(
                    jnp.round(results(peer, j) * factor[j, i : i + 1])
                )
                all_codes[i, t * 2 + j : t * 2 + j + 1, :] = code[j, i : i + 1]

    all_codes[...] = jnp.zeros_like(all_codes)
    for t in range(slabs // 2):
        one_tile(t)
    for i, out in enumerate(outs):
        out[slabs * rows :, :] = to_int16(all_codes[i])


def result_kernel(ks, slabs, skipped, width, *refs):
    count = len(ks)
    ins, (out_ref, buffer, sems) = refs[:count], refs[-3:]
    levels = out_ref.shape[1]
    rows = 2 * levels
    span = slabs // 2 * LANES
    copies = []
    for at, (message, k) in enumerate(zip(ins, ks)):
        scales = scale_of(to_float(message[slabs * rows :, :]), TOP)
        first_col = lax.bitwise_xor(lax.axis_index("rad"), k) * width + skipped
        for half in range(2):
            for pair in range(slabs // 2):
                slab = pair * 2 + half
                for f in range(2):
                    start = slab * rows + f * levels
                    v = to_float(message[start : start + levels, :])
                    buffer[at, half, f, :, pair * LANES : (pair + 1) * LANES] = v * scales[slab : slab + 1, :]
            cols = pl.ds(pl.multiple_of(first_col + half * (width // 2), LANES), span)
            copies.append(pltpu.make_async_copy(buffer.at[at, half], out_ref.at[:, :, cols], sems.at[at, half]))
            copies[-1].start()
    for copy in copies:
        copy.wait()


def send(message, k, groups):
    return message if k == 0 else lax.ppermute(message, "rad", [(i, i ^ k) for i in range(groups)])


def local(slots, nonlin, state, inverse, pair_of_slot):
    levels = nonlin.shape[1]
    groups = lax.axis_size("rad")
    width = nonlin.shape[2] // groups
    size = inverse.shape[-1]
    all_slabs = width // LANES
    half_cols = width // 2
    span = half_cols // CHUNKS
    slabs = 2 * span // LANES
    rows = 2 * levels
    lower_slabs = -(-slots // LANES)
    weights = stencil_table(levels * groups)
    table = jnp.asarray(weights)
    edge_weight = jnp.asarray(np.concatenate([weights[::levels, 0], weights[levels - 1 :: levels, 2]]))
    vmem = pl.BlockSpec(memory_space=pltpu.VMEM)
    hbm = pl.BlockSpec(memory_space=pl.ANY)
    far = list(range(groups // 2, groups))
    near = list(range(groups // 2))
    others = near[1:]
    order = []
    for i, k in enumerate(far):
        order += [k] + others[2 * i : 2 * i + 2]
    order += near[:1]

    def call(kernel, name, flops, moved, vmem_mib, **kwargs):
        return pl.pallas_call(
            kernel,
            name=name,
            compiler_params=pltpu.CompilerParams(vmem_limit_bytes=vmem_mib * MIB),
            cost_estimate=pl.CostEstimate(flops=flops, bytes_accessed=moved, transcendentals=0),
            **kwargs,
        )

    def right_side(ks, chunk, *earlier):
        out_rows = slabs * (rows + EXTRA)
        count = len(ks)
        return call(
            functools.partial(right_side_kernel, ks, slabs, chunk * span, width),
            "right_side",
            MIB * count,
            MIB * count,
            56,
            out_shape=[jax.ShapeDtypeStruct((out_rows, LANES), jnp.int16)] * count,
            in_specs=[hbm] * (3 + len(earlier)),
            out_specs=[hbm] * count,
            scratch_shapes=[
                pltpu.VMEM((count, 2, 2, levels, span), jnp.bfloat16),
                pltpu.VMEM((count, 2, 2, levels, span), jnp.float32),
                pltpu.VMEM((levels, LANES), jnp.float32),
                pltpu.VMEM((count, out_rows, LANES), jnp.int16),
                pltpu.VMEM((slabs * rows, LANES), jnp.float32),
                pltpu.VMEM((slabs, 8, LANES), jnp.float32),
                pltpu.VMEM((slabs, EXTRA, LANES), jnp.float32),
                pltpu.SemaphoreType.DMA((count, 2, 2)),
                pltpu.SemaphoreType.DMA((count + 1,)),
            ],
        )(nonlin, state, table, *earlier)

    def split():
        block = pl.BlockSpec((1, size // 4, size), lambda i, j: (i, j, 0))
        return call(
            split_kernel,
            "split_inverse",
            4 * MIB,
            16 * MIB,
            16,
            out_shape=jax.ShapeDtypeStruct((2, size, 2 * size), jnp.bfloat16),
            grid=(2, 4),
            in_specs=[block],
            out_specs=pl.BlockSpec((1, size // 4, 2 * size), lambda i, j: (i, j, 0)),
        )(inverse[0])

    def product(chunk, messages, both, *earlier):
        return call(
            functools.partial(product_kernel, order, chunk * span // LANES, slabs, lower_slabs),
            "product",
            6 * size * size * slabs * LANES,
            10 * MIB,
            32,
            out_shape=[jax.ShapeDtypeStruct((slabs * rows + TILE, LANES), jnp.int16)] * groups,
            in_specs=[pl.BlockSpec(memory_space=pltpu.SMEM)] * 2
            + [vmem] * (groups + 1)
            + [hbm for _ in earlier],
            out_specs=[vmem] * groups,
            scratch_shapes=2
            * [
                pltpu.VMEM((2 * size, 2 * LANES), jnp.bfloat16),
                pltpu.VMEM((size, 2 * LANES), jnp.float32),
                pltpu.VMEM((groups, 4, 2 * LANES), jnp.float32),
                pltpu.VMEM((2, groups, 8, LANES), jnp.float32),
            ]
            + [pltpu.VMEM((groups, TILE, LANES), jnp.float32)],
        )(pair_of_slot, edge_weight, *messages, both, *earlier)

    def result(ks, chunk, messages, previous):
        carried = [] if previous is None else [previous]
        return call(
            functools.partial(result_kernel, ks, slabs, chunk * span, width),
            "result",
            MIB,
            2 * MIB,
            16,
            out_shape=jax.ShapeDtypeStruct(state.shape, jnp.float32),
            in_specs=[vmem] * len(messages) + [hbm] * len(carried),
            out_specs=hbm,
            scratch_shapes=[
                pltpu.VMEM((len(ks), 2, 2, levels, span), jnp.float32),
                pltpu.SemaphoreType.DMA((len(ks), 2)),
            ],
            input_output_aliases={} if previous is None else {len(ks): 0},
        )(*messages, *carried)

    made, got = [], {}
    for ks, chunk in ((far[:2], 0), (near + far[2:], 0), (far + near, 1)):
        made = right_side(ks, chunk, *made[-1:])
        got.update({(k, chunk): send(m, k, groups) for k, m in zip(ks, made)})
    both = split()
    back, made = [], []
    for chunk in range(CHUNKS):
        made = product(chunk, [got[k, chunk] for k in order], both, *made[-1:])
        back.append({k: send(m, k, groups) for k, m in zip(order, made)})
    out = None
    for chunk, came in enumerate(back):
        for ks in [order] if chunk < CHUNKS - 1 else [order[:4] + order[-1:], order[4:-1]]:
            out = result(ks, chunk, [came[k] for k in ks], out)
    return out


def solution(mesh):
    placed = (
        P(None, "rad", "ang"),
        P(None, "rad", "ang"),
        P(("ang", "rad"), None, None, None),
        P(("ang", "rad")),
    )
    slots = mesh.shape["rad"] * mesh.shape["ang"]
    return jax.shard_map(
        functools.partial(local, slots),
        mesh=mesh,
        in_specs=placed,
        out_specs=P(None, "rad", "ang"),
        check_vma=False,
    )
```

```python
import functools
import math

import jax
import jax.numpy as jnp
import numpy as np
from jax import lax
from jax.experimental import pallas as pl
from jax.experimental.pallas import tpu as pltpu
from jax.sharding import PartitionSpec as P

inner_radius = 0.35
outer_radius = 1.0
blend_weight = 0.5

LANES = 128
EXTRA = 6
CODES = 8
CHUNKS = 2
TOP = 32700.0
EDGE_TOP = 16384.0
FINE = 128.0
MIB = 1024 * 1024


def radius_at(level_index, total_levels):
    scaled = level_index / (total_levels - 1.0)
    stretch = (1.0 - blend_weight) * scaled + blend_weight * (1.0 - np.cos(math.pi * scaled)) / 2.0
    return inner_radius + (outer_radius - inner_radius) * stretch


def stencil_table(total_levels):
    k = np.arange(total_levels, dtype=np.float64)
    radius = radius_at(k, total_levels)
    below = radius - radius_at(k - 1.0, total_levels)
    above = radius_at(k + 1.0, total_levels) - radius
    at_inner, at_outer = k == 0, k == total_levels - 1
    weight_below = np.where(at_inner, 0.0, np.where(at_outer, -1.0 / below, -above / (below * (below + above))))
    weight_here = np.where(
        at_inner, -1.0 / above, np.where(at_outer, 1.0 / below, (above - below) / (below * above))
    )
    weight_above = np.where(at_inner, 1.0 / above, np.where(at_outer, 0.0, below / (above * (below + above))))
    time_step = 0.5 * (outer_radius - inner_radius) / (total_levels - 1.0)
    table = np.zeros((total_levels, LANES), np.float32)
    table[:, 0] = time_step * weight_below
    table[:, 1] = time_step * (weight_here + 2.0 / radius)
    table[:, 2] = time_step * weight_above
    return table


def scale_code(largest, per_octave):
    return jnp.ceil(jnp.log2(jnp.maximum(largest, 1e-30)) * per_octave) * (FINE / per_octave)


def encode_factor(code, top):
    return jnp.exp2(code * (-1.0 / FINE)) * top


def to_int16(values):
    return values.astype(jnp.int32).astype(jnp.int16)


def to_float(codes):
    return codes.astype(jnp.int32).astype(jnp.float32)


def scale_of(codes, top):
    return jnp.exp2(codes * (1.0 / FINE)) * (1.0 / top)


def lanes_of(slab):
    return pl.ds(pl.multiple_of(slab * LANES, LANES), LANES)


def right_side_kernel(ks, slabs, skipped, width, nonlin, state, table, *refs):
    count = len(ks)
    outs, (n_buf, s_buf, tab_buf, messages, values, tops, extra, sems, out_sems) = refs[-9 - count : -9], refs[-9:]
    levels = nonlin.shape[1]
    rows = 2 * levels
    span = slabs // 2 * LANES
    me = lax.axis_index("rad")

    def fetches(at, first):
        made = []
        for half in range(2):
            cols = pl.ds(pl.multiple_of(first + half * (width // 2), LANES), span)
            made.append(pltpu.make_async_copy(nonlin.at[:, :, cols], n_buf.at[at, half], sems.at[at, half, 0]))
            made.append(pltpu.make_async_copy(state.at[:, :, cols], s_buf.at[at, half], sems.at[at, half, 1]))
        return made

    here_rows = pl.ds(pl.multiple_of(me * levels, levels), levels)
    tab_copy = pltpu.make_async_copy(table.at[here_rows, :], tab_buf, out_sems.at[count])
    tab_copy.start()
    for at, k in enumerate(ks):
        for copy in fetches(at, lax.bitwise_xor(me, k) * width + skipped):
            copy.start()
    tab_copy.wait()
    tab = tab_buf[...]
    below, here, above = (jnp.broadcast_to(tab[:, i : i + 1], (levels, LANES)) for i in range(3))
    row = lax.broadcasted_iota(jnp.int32, (levels, LANES), 0)

    def rows_of(slab):
        return pl.ds(pl.multiple_of(slab * rows, rows), rows)

    def one_partner(at, _):
        for copy in fetches(at, 0):
            copy.wait()

        def compute(pair, _):
            cols = lanes_of(pair)
            ends = []
            for half in range(2):
                slab = pair * 2 + half
                top = jnp.zeros((8, LANES), jnp.float32)
                for f in range(2):
                    n = n_buf[at, half, f, :, cols].astype(jnp.float32)
                    prev = jnp.where(row == 0, n, pltpu.roll(n, 1, 0))
                    succ = jnp.where(row == levels - 1, n, pltpu.roll(n, levels - 1, 0))
                    v = s_buf[at, half, f, :, cols] + (below * prev + here * n + above * succ)
                    values[pl.ds(pl.multiple_of(slab * rows + f * levels, levels), levels), :] = v
                    top = jnp.maximum(top, jnp.max(jnp.abs(v).reshape(levels // 8, 8, LANES), axis=0))
                    ends += [n[:1], n[levels - 1 :]]
                tops[slab] = top
            extra[pair] = jnp.concatenate(ends, axis=0)
            return 0

        lax.fori_loop(0, slabs // 2, compute, 0)
        ends = extra[...]
        code = scale_code(jnp.max(tops[...], axis=1), FINE)
        factor = encode_factor(code, TOP)
        edge_codes = [scale_code(jnp.max(jnp.abs(e), axis=1), 1.0) for e in (ends[:, :4], ends[:, 4:])]
        edge_factors = [encode_factor(c, EDGE_TOP)[:, None, :] for c in edge_codes]
        at_row = lax.broadcasted_iota(jnp.int32, ends.shape, 1)
        ends = jnp.round(ends * jnp.where(at_row < 4, *edge_factors))
        messages[at, slabs * rows :, :] = to_int16(
            jnp.concatenate([ends.reshape(slabs * 4, LANES), *edge_codes, code], axis=0)
        )
        tops[:, 0, :] = factor

        def code_slab(slab, _):
            messages[at, rows_of(slab), :] = to_int16(jnp.round(values[rows_of(slab), :] * tops[slab, 0:1, :]))
            return 0

        lax.fori_loop(0, slabs, code_slab, 0, unroll=2)
        for i, out in enumerate(outs):

            @pl.when(at == i)
            def _():
                pltpu.make_async_copy(messages.at[i], out, out_sems.at[i]).start()

        return 0

    lax.fori_loop(0, count, one_partner, 0)
    for i, out in enumerate(outs):
        pltpu.make_async_copy(messages.at[i], out, out_sems.at[i]).wait()


def split_kernel(a_ref, both_ref):
    a = a_ref[...]
    size = a.shape[-1]
    hi = a.astype(jnp.bfloat16)
    both_ref[:, :, size:] = hi
    both_ref[:, :, :size] = (a - hi.astype(jnp.float32)).astype(jnp.bfloat16)


def swapped(edges):
    return jnp.concatenate([edges[1:2], edges[0:1], edges[3:4], edges[2:3]], axis=0)


def product_kernel(order, first_slab, slabs, lower_slabs, pair_ref, edge_weight, *refs):
    groups = len(order)
    ins, both_ref = refs[:groups], refs[groups]
    outs, scratch, all_codes = refs[-groups - 9 : -9], refs[-9:-1], refs[-1]
    size = both_ref.shape[1]
    levels = size // (2 * groups)
    rows = 2 * levels
    me = lax.axis_index("rad")
    pair = pair_ref[0]
    peers = [lax.bitwise_xor(me, k) for k in order]
    near = lax.broadcasted_iota(jnp.int32, (8, LANES), 0)

    def place(f, peer):
        return pl.ds(pl.multiple_of(f * (size // 2) + peer * levels, levels), levels)

    def one_tile(t):
        v_both, y, edges, codes = scratch[t % 2 * 4 : t % 2 * 4 + 4]
        extras = []
        for ref, peer in zip(ins, peers):
            extra = to_float(ref[slabs * rows :, :])
            power = jnp.exp2(extra[4 * slabs :] * (1.0 / FINE))
            extras.append(power[slabs + 2 * t : slabs + 2 * t + 2] * (1.0 / TOP))
            for j in range(2):
                at = t * 8 + j * 4
                code = j * (slabs // 2) + t
                edges[peer, :, j * LANES : (j + 1) * LANES] = extra[at : at + 4] * (
                    power[code : code + 1] * (1.0 / EDGE_TOP)
                )
        for ref, peer, scales in zip(ins, peers, extras):
            before, after = jnp.maximum(peer - 1, 0), jnp.minimum(peer + 1, groups - 1)
            weight_before, weight_after = edge_weight[peer], edge_weight[groups + peer]
            for j in range(2):
                cols = slice(j * LANES, (j + 1) * LANES)
                scale = scales[j : j + 1]
                here = swapped(edges[peer, :, cols])
                low = weight_before * (edges[before, :, cols] - here)
                high = weight_after * (edges[after, :, cols] - here)
                start = (t * 2 + j) * rows
                for f in range(2):
                    v = to_float(ref[start + f * levels : start + (f + 1) * levels, :]) * scale
                    first = v[:8] + jnp.where(near == 0, low[2 * f + 1 : 2 * f + 2], 0.0)
                    last = v[levels - 8 :] + jnp.where(near == 7, high[2 * f : 2 * f + 1], 0.0)
                    middle = [v[8 : levels - 8]] if levels > 16 else []
                    v = jnp.concatenate([first] + middle + [last], axis=0)
                    hi = v.astype(jnp.bfloat16)
                    v_both[place(f, peer), cols] = hi
                    v_both[place(f + 2, peer), cols] = (v - hi.astype(jnp.float32)).astype(jnp.bfloat16)

        def product(which):
            dot = functools.partial(jnp.dot, preferred_element_type=jnp.float32)
            return dot(both_ref[which], v_both[...]) + dot(both_ref[which, :, size:], v_both[:size, :])

        upper = product(1)
        if first_slab + t < lower_slabs:
            lane = lax.broadcasted_iota(jnp.int32, upper.shape, 1)
            column = (first_slab + t) * LANES + jnp.where(lane < LANES, lane, lane - LANES + 1)
            y[...] = jnp.where(column < pair + 1, product(0), upper)
        else:
            y[...] = upper

        def results(peer, j):
            return jnp.concatenate([y[place(f, peer), j * LANES : (j + 1) * LANES] for f in range(2)], axis=0)

        for i, peer in enumerate(peers):
            for j in range(2):
                v = jnp.abs(results(peer, j))
                codes[j, i] = jnp.max(v.reshape(rows // 8, 8, LANES), axis=0)
        code = scale_code(jnp.max(codes[...], axis=2), FINE)
        factor = encode_factor(code, TOP)
        for i, (out, peer) in enumerate(zip(outs, peers)):
            for j in range(2):
                start = (t * 2 + j) * rows
                out[start : start + rows, :] = to_int16(
                    jnp.round(results(peer, j) * factor[j, i : i + 1])
                )
                all_codes[i, t * 2 + j : t * 2 + j + 1, :] = code[j, i : i + 1]

    all_codes[...] = jnp.zeros_like(all_codes)
    for t in range(slabs // 2):
        one_tile(t)
    for i, out in enumerate(outs):
        out[slabs * rows :, :] = to_int16(all_codes[i])


def result_kernel(ks, slabs, skipped, width, *refs):
    count = len(ks)
    ins, (out_ref, buffer, sems) = refs[:count], refs[-3:]
    levels = out_ref.shape[1]
    rows = 2 * levels
    span = slabs // 2 * LANES
    copies = []
    for at, (message, k) in enumerate(zip(ins, ks)):
        scales = scale_of(to_float(message[slabs * rows :, :]), TOP)
        first_col = lax.bitwise_xor(lax.axis_index("rad"), k) * width + skipped
        for half in range(2):
            for pair in range(slabs // 2):
                slab = pair * 2 + half
                for f in range(2):
                    start = slab * rows + f * levels
                    v = to_float(message[start : start + levels, :])
                    buffer[at, half, f, :, pair * LANES : (pair + 1) * LANES] = v * scales[slab : slab + 1, :]
            cols = pl.ds(pl.multiple_of(first_col + half * (width // 2), LANES), span)
            copies.append(pltpu.make_async_copy(buffer.at[at, half], out_ref.at[:, :, cols], sems.at[at, half]))
            copies[-1].start()
    for copy in copies:
        copy.wait()


def send(message, k, groups):
    return message if k == 0 else lax.ppermute(message, "rad", [(i, i ^ k) for i in range(groups)])


def local(slots, nonlin, state, inverse, pair_of_slot):
    levels = nonlin.shape[1]
    groups = lax.axis_size("rad")
    width = nonlin.shape[2] // groups
    size = inverse.shape[-1]
    all_slabs = width // LANES
    half_cols = width // 2
    span = half_cols // CHUNKS
    slabs = 2 * span // LANES
    rows = 2 * levels
    lower_slabs = -(-slots // LANES)
    weights = stencil_table(levels * groups)
    table = jnp.asarray(weights)
    edge_weight = jnp.asarray(np.concatenate([weights[::levels, 0], weights[levels - 1 :: levels, 2]]))
    vmem = pl.BlockSpec(memory_space=pltpu.VMEM)
    hbm = pl.BlockSpec(memory_space=pl.ANY)
    far = list(range(groups // 2, groups))
    near = list(range(groups // 2))
    others = near[1:]
    order = []
    for i, k in enumerate(far):
        order += [k] + others[2 * i : 2 * i + 2]
    order += near[:1]

    def call(kernel, name, flops, moved, vmem_mib, **kwargs):
        return pl.pallas_call(
            kernel,
            name=name,
            compiler_params=pltpu.CompilerParams(vmem_limit_bytes=vmem_mib * MIB),
            cost_estimate=pl.CostEstimate(flops=flops, bytes_accessed=moved, transcendentals=0),
            **kwargs,
        )

    def right_side(ks, chunk, *earlier):
        out_rows = slabs * (rows + EXTRA)
        count = len(ks)
        return call(
            functools.partial(right_side_kernel, ks, slabs, chunk * span, width),
            "right_side",
            MIB * count,
            MIB * count,
            56,
            out_shape=[jax.ShapeDtypeStruct((out_rows, LANES), jnp.int16)] * count,
            in_specs=[hbm] * (3 + len(earlier)),
            out_specs=[hbm] * count,
            scratch_shapes=[
                pltpu.VMEM((count, 2, 2, levels, span), jnp.bfloat16),
                pltpu.VMEM((count, 2, 2, levels, span), jnp.float32),
                pltpu.VMEM((levels, LANES), jnp.float32),
                pltpu.VMEM((count, out_rows, LANES), jnp.int16),
                pltpu.VMEM((slabs * rows, LANES), jnp.float32),
                pltpu.VMEM((slabs, 8, LANES), jnp.float32),
                pltpu.VMEM((slabs // 2, 8, LANES), jnp.float32),
                pltpu.SemaphoreType.DMA((count, 2, 2)),
                pltpu.SemaphoreType.DMA((count + 1,)),
            ],
        )(nonlin, state, table, *earlier)

    def split():
        block = pl.BlockSpec((1, size // 4, size), lambda i, j: (i, j, 0))
        return call(
            split_kernel,
            "split_inverse",
            4 * MIB,
            16 * MIB,
            16,
            out_shape=jax.ShapeDtypeStruct((2, size, 2 * size), jnp.bfloat16),
            grid=(2, 4),
            in_specs=[block],
            out_specs=pl.BlockSpec((1, size // 4, 2 * size), lambda i, j: (i, j, 0)),
        )(inverse[0])

    def product(chunk, messages, both, *earlier):
        return call(
            functools.partial(product_kernel, order, chunk * span // LANES, slabs, lower_slabs),
            "product",
            6 * size * size * slabs * LANES,
            10 * MIB,
            32,
            out_shape=[jax.ShapeDtypeStruct((slabs * rows + CODES, LANES), jnp.int16)] * groups,
            in_specs=[pl.BlockSpec(memory_space=pltpu.SMEM)] * 2
            + [vmem] * (groups + 1)
            + [hbm for _ in earlier],
            out_specs=[vmem] * groups,
            scratch_shapes=2
            * [
                pltpu.VMEM((2 * size, 2 * LANES), jnp.bfloat16),
                pltpu.VMEM((size, 2 * LANES), jnp.float32),
                pltpu.VMEM((groups, 4, 2 * LANES), jnp.float32),
                pltpu.VMEM((2, groups, 8, LANES), jnp.float32),
            ]
            + [pltpu.VMEM((groups, CODES, LANES), jnp.float32)],
        )(pair_of_slot, edge_weight, *messages, both, *earlier)

    def result(ks, chunk, messages, previous):
        carried = [] if previous is None else [previous]
        return call(
            functools.partial(result_kernel, ks, slabs, chunk * span, width),
            "result",
            MIB,
            2 * MIB,
            16,
            out_shape=jax.ShapeDtypeStruct(state.shape, jnp.float32),
            in_specs=[vmem] * len(messages) + [hbm] * len(carried),
            out_specs=hbm,
            scratch_shapes=[
                pltpu.VMEM((len(ks), 2, 2, levels, span), jnp.float32),
                pltpu.SemaphoreType.DMA((len(ks), 2)),
            ],
            input_output_aliases={} if previous is None else {len(ks): 0},
        )(*messages, *carried)

    made, got = [], {}
    for ks, chunk in ((far[:2], 0), (near + far[2:], 0), (far + near, 1)):
        made = right_side(ks, chunk, *made[-1:])
        got.update({(k, chunk): send(m, k, groups) for k, m in zip(ks, made)})
    both = split()
    back, made = [], []
    for chunk in range(CHUNKS):
        made = product(chunk, [got[k, chunk] for k in order], both, *made[-1:])
        back.append({k: send(m, k, groups) for k, m in zip(order, made)})
    out = None
    for chunk, came in enumerate(back):
        for ks in [order] if chunk < CHUNKS - 1 else [order[:4] + order[-1:], order[4:-1]]:
            out = result(ks, chunk, [came[k] for k in ks], out)
    return out


def solution(mesh):
    placed = (
        P(None, "rad", "ang"),
        P(None, "rad", "ang"),
        P(("ang", "rad"), None, None, None),
        P(("ang", "rad")),
    )
    slots = mesh.shape["rad"] * mesh.shape["ang"]
    return jax.shard_map(
        functools.partial(local, slots),
        mesh=mesh,
        in_specs=placed,
        out_specs=P(None, "rad", "ang"),
        check_vma=False,
    )
```

```python
import functools
import math

import jax
import jax.numpy as jnp
import numpy as np
from jax import lax
from jax.experimental import pallas as pl
from jax.experimental.pallas import tpu as pltpu
from jax.sharding import PartitionSpec as P

inner_radius = 0.35
outer_radius = 1.0
blend_weight = 0.5

LANES = 128
EXTRA = 6
CODES = 8
CHUNKS = 2
TOP = 32700.0
EDGE_TOP = 16384.0
FINE = 128.0
MIB = 1024 * 1024


def radius_at(level_index, total_levels):
    scaled = level_index / (total_levels - 1.0)
    stretch = (1.0 - blend_weight) * scaled + blend_weight * (1.0 - np.cos(math.pi * scaled)) / 2.0
    return inner_radius + (outer_radius - inner_radius) * stretch


def stencil_table(total_levels):
    k = np.arange(total_levels, dtype=np.float64)
    radius = radius_at(k, total_levels)
    below = radius - radius_at(k - 1.0, total_levels)
    above = radius_at(k + 1.0, total_levels) - radius
    at_inner, at_outer = k == 0, k == total_levels - 1
    weight_below = np.where(at_inner, 0.0, np.where(at_outer, -1.0 / below, -above / (below * (below + above))))
    weight_here = np.where(
        at_inner, -1.0 / above, np.where(at_outer, 1.0 / below, (above - below) / (below * above))
    )
    weight_above = np.where(at_inner, 1.0 / above, np.where(at_outer, 0.0, below / (above * (below + above))))
    time_step = 0.5 * (outer_radius - inner_radius) / (total_levels - 1.0)
    table = np.zeros((total_levels, LANES), np.float32)
    table[:, 0] = time_step * weight_below
    table[:, 1] = time_step * (weight_here + 2.0 / radius)
    table[:, 2] = time_step * weight_above
    return table


def scale_code(largest, per_octave):
    return jnp.ceil(jnp.log2(jnp.maximum(largest, 1e-30)) * per_octave) * (FINE / per_octave)


def encode_factor(code, top):
    return jnp.exp2(code * (-1.0 / FINE)) * top


def to_int16(values):
    return values.astype(jnp.int32).astype(jnp.int16)


def to_float(codes):
    return codes.astype(jnp.int32).astype(jnp.float32)


def scale_of(codes, top):
    return jnp.exp2(codes * (1.0 / FINE)) * (1.0 / top)


def lanes_of(slab):
    return pl.ds(pl.multiple_of(slab * LANES, LANES), LANES)


def right_side_kernel(ks, slabs, skipped, width, nonlin, state, table, *refs):
    count = len(ks)
    outs, (n_buf, s_buf, tab_buf, messages, values, tops, extra, sems, out_sems) = refs[-9 - count : -9], refs[-9:]
    levels = nonlin.shape[1]
    rows = 2 * levels
    span = slabs // 2 * LANES
    me = lax.axis_index("rad")

    def fetches(at, first):
        made = []
        for half in range(2):
            cols = pl.ds(pl.multiple_of(first + half * (width // 2), LANES), span)
            made.append(pltpu.make_async_copy(nonlin.at[:, :, cols], n_buf.at[at, half], sems.at[at, half, 0]))
            made.append(pltpu.make_async_copy(state.at[:, :, cols], s_buf.at[at, half], sems.at[at, half, 1]))
        return made

    here_rows = pl.ds(pl.multiple_of(me * levels, levels), levels)
    tab_copy = pltpu.make_async_copy(table.at[here_rows, :], tab_buf, out_sems.at[count])
    tab_copy.start()
    for at, k in enumerate(ks):
        for copy in fetches(at, lax.bitwise_xor(me, k) * width + skipped):
            copy.start()
    tab_copy.wait()
    tab = tab_buf[...]
    below, here, above = (jnp.broadcast_to(tab[:, i : i + 1], (levels, LANES)) for i in range(3))
    row = lax.broadcasted_iota(jnp.int32, (levels, LANES), 0)

    def rows_of(slab):
        return pl.ds(pl.multiple_of(slab * rows, rows), rows)

    def one_partner(at, _):
        for copy in fetches(at, 0):
            copy.wait()

        def compute(pair, _):
            cols = lanes_of(pair)
            ends = []
            for half in range(2):
                slab = pair * 2 + half
                top = jnp.zeros((8, LANES), jnp.float32)
                for f in range(2):
                    n = n_buf[at, half, f, :, cols].astype(jnp.float32)
                    prev = jnp.where(row == 0, n, pltpu.roll(n, 1, 0))
                    succ = jnp.where(row == levels - 1, n, pltpu.roll(n, levels - 1, 0))
                    v = s_buf[at, half, f, :, cols] + (below * prev + here * n + above * succ)
                    values[pl.ds(pl.multiple_of(slab * rows + f * levels, levels), levels), :] = v
                    top = jnp.maximum(top, jnp.max(jnp.abs(v).reshape(levels // 8, 8, LANES), axis=0))
                    ends += [n[:1], n[levels - 1 :]]
                tops[slab] = top
            extra[pair] = jnp.concatenate(ends, axis=0)
            return 0

        lax.fori_loop(0, slabs // 2, compute, 0)
        ends = extra[...]
        code = scale_code(jnp.max(tops[...], axis=1), FINE)
        factor = encode_factor(code, TOP)
        edge_codes = [scale_code(jnp.max(jnp.abs(e), axis=1), 1.0) for e in (ends[:, :4], ends[:, 4:])]
        edge_factors = [encode_factor(c, EDGE_TOP)[:, None, :] for c in edge_codes]
        at_row = lax.broadcasted_iota(jnp.int32, ends.shape, 1)
        ends = jnp.round(ends * jnp.where(at_row < 4, *edge_factors))
        messages[at, slabs * rows :, :] = to_int16(
            jnp.concatenate([ends.reshape(slabs * 4, LANES), *edge_codes, code], axis=0)
        )
        tops[:, 0, :] = factor

        def code_slab(slab, _):
            messages[at, rows_of(slab), :] = to_int16(jnp.round(values[rows_of(slab), :] * tops[slab, 0:1, :]))
            return 0

        lax.fori_loop(0, slabs, code_slab, 0, unroll=2)
        for i, out in enumerate(outs):

            @pl.when(at == i)
            def _():
                pltpu.make_async_copy(messages.at[i], out, out_sems.at[i]).start()

        return 0

    lax.fori_loop(0, count, one_partner, 0)
    for i, out in enumerate(outs):
        pltpu.make_async_copy(messages.at[i], out, out_sems.at[i]).wait()


def split_kernel(a_ref, both_ref):
    a = a_ref[...]
    size = a.shape[-1]
    hi = a.astype(jnp.bfloat16)
    both_ref[:, :, size:] = hi
    both_ref[:, :, :size] = (a - hi.astype(jnp.float32)).astype(jnp.bfloat16)


def swapped(edges):
    return jnp.concatenate([edges[1:2], edges[0:1], edges[3:4], edges[2:3]], axis=0)


def product_kernel(order, first_slab, slabs, lower_slabs, pair_ref, edge_weight, *refs):
    groups = len(order)
    ins, both_ref = refs[:groups], refs[groups]
    outs, scratch, all_codes = refs[-groups - 9 : -9], refs[-9:-1], refs[-1]
    size = both_ref.shape[1]
    levels = size // (2 * groups)
    rows = 2 * levels
    me = lax.axis_index("rad")
    pair = pair_ref[0]
    peers = [lax.bitwise_xor(me, k) for k in order]
    near = lax.broadcasted_iota(jnp.int32, (8, LANES), 0)

    def place(f, peer):
        return pl.ds(pl.multiple_of(f * (size // 2) + peer * levels, levels), levels)

    def one_tile(t):
        v_both, y, edges, codes = scratch[t % 2 * 4 : t % 2 * 4 + 4]
        extras = []
        for ref, peer in zip(ins, peers):
            extra = to_float(ref[slabs * rows :, :])
            power = jnp.exp2(extra[4 * slabs :] * (1.0 / FINE))
            extras.append(power[slabs + 2 * t : slabs + 2 * t + 2] * (1.0 / TOP))
            for j in range(2):
                at = t * 8 + j * 4
                code = j * (slabs // 2) + t
                edges[peer, :, j * LANES : (j + 1) * LANES] = extra[at : at + 4] * (
                    power[code : code + 1] * (1.0 / EDGE_TOP)
                )
        for ref, peer, scales in zip(ins, peers, extras):
            before, after = jnp.maximum(peer - 1, 0), jnp.minimum(peer + 1, groups - 1)
            weight_before, weight_after = edge_weight[peer], edge_weight[groups + peer]
            for j in range(2):
                cols = slice(j * LANES, (j + 1) * LANES)
                scale = scales[j : j + 1]
                here = swapped(edges[peer, :, cols])
                low = weight_before * (edges[before, :, cols] - here)
                high = weight_after * (edges[after, :, cols] - here)
                start = (t * 2 + j) * rows
                for f in range(2):
                    v = to_float(ref[start + f * levels : start + (f + 1) * levels, :]) * scale
                    first = v[:8] + jnp.where(near == 0, low[2 * f + 1 : 2 * f + 2], 0.0)
                    last = v[levels - 8 :] + jnp.where(near == 7, high[2 * f : 2 * f + 1], 0.0)
                    middle = [v[8 : levels - 8]] if levels > 16 else []
                    v = jnp.concatenate([first] + middle + [last], axis=0)
                    hi = v.astype(jnp.bfloat16)
                    v_both[place(f, peer), cols] = hi
                    v_both[place(f + 2, peer), cols] = (v - hi.astype(jnp.float32)).astype(jnp.bfloat16)

        def product(which):
            dot = functools.partial(jnp.dot, preferred_element_type=jnp.float32)
            return dot(both_ref[which], v_both[...]) + dot(both_ref[which, :, size:], v_both[:size, :])

        upper = product(1)
        if first_slab + t < lower_slabs:
            lane = lax.broadcasted_iota(jnp.int32, upper.shape, 1)
            column = (first_slab + t) * LANES + jnp.where(lane < LANES, lane, lane - LANES + 1)
            y[...] = jnp.where(column < pair + 1, product(0), upper)
        else:
            y[...] = upper

        def results(peer, j):
            return jnp.concatenate([y[place(f, peer), j * LANES : (j + 1) * LANES] for f in range(2)], axis=0)

        for i, peer in enumerate(peers):
            for j in range(2):
                v = jnp.abs(results(peer, j))
                codes[j, i] = jnp.max(v.reshape(rows // 8, 8, LANES), axis=0)
        code = scale_code(jnp.max(codes[...], axis=2), FINE)
        factor = encode_factor(code, TOP)
        for i, (out, peer) in enumerate(zip(outs, peers)):
            for j in range(2):
                start = (t * 2 + j) * rows
                out[start : start + rows, :] = to_int16(
                    jnp.round(results(peer, j) * factor[j, i : i + 1])
                )
                all_codes[i, t * 2 + j : t * 2 + j + 1, :] = code[j, i : i + 1]

    all_codes[...] = jnp.zeros_like(all_codes)
    for t in range(slabs // 2):
        one_tile(t)
    for i, out in enumerate(outs):
        out[slabs * rows :, :] = to_int16(all_codes[i])


def result_kernel(ks, slabs, skipped, width, *refs):
    count = len(ks)
    ins, (out_ref, buffer, sems) = refs[:count], refs[-3:]
    levels = out_ref.shape[1]
    rows = 2 * levels
    span = slabs // 2 * LANES
    copies = []
    for at, (message, k) in enumerate(zip(ins, ks)):
        scales = scale_of(to_float(message[slabs * rows :, :]), TOP)
        first_col = lax.bitwise_xor(lax.axis_index("rad"), k) * width + skipped
        for half in range(2):
            for pair in range(slabs // 2):
                slab = pair * 2 + half
                for f in range(2):
                    start = slab * rows + f * levels
                    v = to_float(message[start : start + levels, :])
                    buffer[at, half, f, :, pair * LANES : (pair + 1) * LANES] = v * scales[slab : slab + 1, :]
            cols = pl.ds(pl.multiple_of(first_col + half * (width // 2), LANES), span)
            copies.append(pltpu.make_async_copy(buffer.at[at, half], out_ref.at[:, :, cols], sems.at[at, half]))
            copies[-1].start()
    for copy in copies:
        copy.wait()


def send(message, k, groups):
    return message if k == 0 else lax.ppermute(message, "rad", [(i, i ^ k) for i in range(groups)])


def local(slots, nonlin, state, inverse, pair_of_slot):
    levels = nonlin.shape[1]
    groups = lax.axis_size("rad")
    width = nonlin.shape[2] // groups
    size = inverse.shape[-1]
    all_slabs = width // LANES
    half_cols = width // 2
    span = half_cols // CHUNKS
    slabs = 2 * span // LANES
    rows = 2 * levels
    lower_slabs = -(-slots // LANES)
    weights = stencil_table(levels * groups)
    table = jnp.asarray(weights)
    edge_weight = jnp.asarray(np.concatenate([weights[::levels, 0], weights[levels - 1 :: levels, 2]]))
    vmem = pl.BlockSpec(memory_space=pltpu.VMEM)
    hbm = pl.BlockSpec(memory_space=pl.ANY)
    far = list(range(groups // 2, groups))
    near = list(range(groups // 2))
    others = near[1:]
    order = []
    for i, k in enumerate(far):
        order += [k] + others[2 * i : 2 * i + 2]
    order += near[:1]
    in_turn = [k for both in zip(far, others) for k in both] + far[-1:] + near[:1]

    def call(kernel, name, flops, moved, vmem_mib, **kwargs):
        return pl.pallas_call(
            kernel,
            name=name,
            compiler_params=pltpu.CompilerParams(vmem_limit_bytes=vmem_mib * MIB),
            cost_estimate=pl.CostEstimate(flops=flops, bytes_accessed=moved, transcendentals=0),
            **kwargs,
        )

    def right_side(ks, chunk, *earlier):
        out_rows = slabs * (rows + EXTRA)
        count = len(ks)
        return call(
            functools.partial(right_side_kernel, ks, slabs, chunk * span, width),
            "right_side",
            MIB * count,
            MIB * count,
            56,
            out_shape=[jax.ShapeDtypeStruct((out_rows, LANES), jnp.int16)] * count,
            in_specs=[hbm] * (3 + len(earlier)),
            out_specs=[hbm] * count,
            scratch_shapes=[
                pltpu.VMEM((count, 2, 2, levels, span), jnp.bfloat16),
                pltpu.VMEM((count, 2, 2, levels, span), jnp.float32),
                pltpu.VMEM((levels, LANES), jnp.float32),
                pltpu.VMEM((count, out_rows, LANES), jnp.int16),
                pltpu.VMEM((slabs * rows, LANES), jnp.float32),
                pltpu.VMEM((slabs, 8, LANES), jnp.float32),
                pltpu.VMEM((slabs // 2, 8, LANES), jnp.float32),
                pltpu.SemaphoreType.DMA((count, 2, 2)),
                pltpu.SemaphoreType.DMA((count + 1,)),
            ],
        )(nonlin, state, table, *earlier)

    def split():
        block = pl.BlockSpec((1, size // 4, size), lambda i, j: (i, j, 0))
        return call(
            split_kernel,
            "split_inverse",
            4 * MIB,
            16 * MIB,
            16,
            out_shape=jax.ShapeDtypeStruct((2, size, 2 * size), jnp.bfloat16),
            grid=(2, 4),
            in_specs=[block],
            out_specs=pl.BlockSpec((1, size // 4, 2 * size), lambda i, j: (i, j, 0)),
        )(inverse[0])

    def product(chunk, messages, both, *earlier):
        return call(
            functools.partial(product_kernel, order, chunk * span // LANES, slabs, lower_slabs),
            "product",
            6 * size * size * slabs * LANES,
            10 * MIB,
            32,
            out_shape=[jax.ShapeDtypeStruct((slabs * rows + CODES, LANES), jnp.int16)] * groups,
            in_specs=[pl.BlockSpec(memory_space=pltpu.SMEM)] * 2
            + [vmem] * (groups + 1)
            + [hbm for _ in earlier],
            out_specs=[vmem] * groups,
            scratch_shapes=2
            * [
                pltpu.VMEM((2 * size, 2 * LANES), jnp.bfloat16),
                pltpu.VMEM((size, 2 * LANES), jnp.float32),
                pltpu.VMEM((groups, 4, 2 * LANES), jnp.float32),
                pltpu.VMEM((2, groups, 8, LANES), jnp.float32),
            ]
            + [pltpu.VMEM((groups, CODES, LANES), jnp.float32)],
        )(pair_of_slot, edge_weight, *messages, both, *earlier)

    def result(ks, chunk, messages, previous):
        carried = [] if previous is None else [previous]
        return call(
            functools.partial(result_kernel, ks, slabs, chunk * span, width),
            "result",
            MIB,
            2 * MIB,
            16,
            out_shape=jax.ShapeDtypeStruct(state.shape, jnp.float32),
            in_specs=[vmem] * len(messages) + [hbm] * len(carried),
            out_specs=hbm,
            scratch_shapes=[
                pltpu.VMEM((len(ks), 2, 2, levels, span), jnp.float32),
                pltpu.SemaphoreType.DMA((len(ks), 2)),
            ],
            input_output_aliases={} if previous is None else {len(ks): 0},
        )(*messages, *carried)

    made, got = [], {}
    for ks, chunk in ((far[:2], 0), (near + far[2:], 0), (far + near, 1)):
        made = right_side(ks, chunk, *made[-1:])
        got.update({(k, chunk): send(m, k, groups) for k, m in zip(ks, made)})
    both = split()
    back, made = [], []
    for chunk in range(CHUNKS):
        made = product(chunk, [got[k, chunk] for k in order], both, *made[-1:])
        back.append({k: send(m, k, groups) for k, m in zip(order, made)})
    out = None
    for chunk, came in enumerate(back):
        for ks in [in_turn] if chunk < CHUNKS - 1 else [far[:1] + others + near[:1], far[1:]]:
            out = result(ks, chunk, [came[k] for k in ks], out)
    return out


def solution(mesh):
    placed = (
        P(None, "rad", "ang"),
        P(None, "rad", "ang"),
        P(("ang", "rad"), None, None, None),
        P(("ang", "rad")),
    )
    slots = mesh.shape["rad"] * mesh.shape["ang"]
    return jax.shard_map(
        functools.partial(local, slots),
        mesh=mesh,
        in_specs=placed,
        out_specs=P(None, "rad", "ang"),
        check_vma=False,
    )
```

```python
import functools
import math

import jax
import jax.numpy as jnp
import numpy as np
from jax import lax
from jax.experimental import pallas as pl
from jax.experimental.pallas import tpu as pltpu
from jax.sharding import PartitionSpec as P

inner_radius = 0.35
outer_radius = 1.0
blend_weight = 0.5

LANES = 128
EXTRA = 6
CODES = 8
CHUNKS = 2
TOP = 32700.0
EDGE_TOP = 16384.0
FINE = 128.0
MIB = 1024 * 1024


def radius_at(level_index, total_levels):
    scaled = level_index / (total_levels - 1.0)
    stretch = (1.0 - blend_weight) * scaled + blend_weight * (1.0 - np.cos(math.pi * scaled)) / 2.0
    return inner_radius + (outer_radius - inner_radius) * stretch


def stencil_table(total_levels):
    k = np.arange(total_levels, dtype=np.float64)
    radius = radius_at(k, total_levels)
    below = radius - radius_at(k - 1.0, total_levels)
    above = radius_at(k + 1.0, total_levels) - radius
    at_inner, at_outer = k == 0, k == total_levels - 1
    weight_below = np.where(at_inner, 0.0, np.where(at_outer, -1.0 / below, -above / (below * (below + above))))
    weight_here = np.where(
        at_inner, -1.0 / above, np.where(at_outer, 1.0 / below, (above - below) / (below * above))
    )
    weight_above = np.where(at_inner, 1.0 / above, np.where(at_outer, 0.0, below / (above * (below + above))))
    time_step = 0.5 * (outer_radius - inner_radius) / (total_levels - 1.0)
    table = np.zeros((total_levels, LANES), np.float32)
    table[:, 0] = time_step * weight_below
    table[:, 1] = time_step * (weight_here + 2.0 / radius)
    table[:, 2] = time_step * weight_above
    return table


def scale_code(largest, per_octave):
    return jnp.ceil(jnp.log2(jnp.maximum(largest, 1e-30)) * per_octave) * (FINE / per_octave)


def encode_factor(code, top):
    return jnp.exp2(code * (-1.0 / FINE)) * top


def to_int16(values):
    return values.astype(jnp.int32).astype(jnp.int16)


def to_float(codes):
    return codes.astype(jnp.int32).astype(jnp.float32)


def scale_of(codes, top):
    return jnp.exp2(codes * (1.0 / FINE)) * (1.0 / top)


def lanes_of(slab):
    return pl.ds(pl.multiple_of(slab * LANES, LANES), LANES)


def right_side_kernel(ks, slabs, skipped, width, nonlin, state, table, *refs):
    count = len(ks)
    outs, (n_buf, s_buf, tab_buf, messages, values, tops, extra, sems, out_sems) = refs[-9 - count : -9], refs[-9:]
    levels = nonlin.shape[1]
    rows = 2 * levels
    span = slabs // 2 * LANES
    me = lax.axis_index("rad")

    def fetches(at, first):
        made = []
        for half in range(2):
            cols = pl.ds(pl.multiple_of(first + half * (width // 2), LANES), span)
            made.append(pltpu.make_async_copy(nonlin.at[:, :, cols], n_buf.at[at, half], sems.at[at, half, 0]))
            made.append(pltpu.make_async_copy(state.at[:, :, cols], s_buf.at[at, half], sems.at[at, half, 1]))
        return made

    here_rows = pl.ds(pl.multiple_of(me * levels, levels), levels)
    tab_copy = pltpu.make_async_copy(table.at[here_rows, :], tab_buf, out_sems.at[count])
    tab_copy.start()
    for at, k in enumerate(ks):
        for copy in fetches(at, lax.bitwise_xor(me, k) * width + skipped):
            copy.start()
    tab_copy.wait()
    tab = tab_buf[...]
    below, here, above = (jnp.broadcast_to(tab[:, i : i + 1], (levels, LANES)) for i in range(3))
    row = lax.broadcasted_iota(jnp.int32, (8, LANES), 0)

    def rows_of(slab):
        return pl.ds(pl.multiple_of(slab * rows, rows), rows)

    def one_partner(at, _):
        for copy in fetches(at, 0):
            copy.wait()

        def compute(pair, _):
            cols = lanes_of(pair)
            ends = []
            for half in range(2):
                slab = pair * 2 + half
                top = jnp.zeros((8, LANES), jnp.float32)
                for f in range(2):
                    n = n_buf[at, half, f, :, cols].astype(jnp.float32)
                    prev, succ = pltpu.roll(n, 1, 0), pltpu.roll(n, levels - 1, 0)
                    prev = jnp.concatenate([jnp.where(row == 0, n[:8], prev[:8]), prev[8:]], axis=0)
                    succ = jnp.concatenate([succ[:-8], jnp.where(row == 7, n[-8:], succ[-8:])], axis=0)
                    v = s_buf[at, half, f, :, cols] + (below * prev + here * n + above * succ)
                    values[pl.ds(pl.multiple_of(slab * rows + f * levels, levels), levels), :] = v
                    top = jnp.maximum(top, jnp.max(jnp.abs(v).reshape(levels // 8, 8, LANES), axis=0))
                    ends += [n[:1], n[levels - 1 :]]
                tops[slab] = top
            extra[pair] = jnp.concatenate(ends, axis=0)
            return 0

        lax.fori_loop(0, slabs // 2, compute, 0)
        ends = extra[...]
        code = scale_code(jnp.max(tops[...], axis=1), FINE)
        factor = encode_factor(code, TOP)
        edge_codes = [scale_code(jnp.max(jnp.abs(e), axis=1), 1.0) for e in (ends[:, :4], ends[:, 4:])]
        edge_factors = [encode_factor(c, EDGE_TOP)[:, None, :] for c in edge_codes]
        at_row = lax.broadcasted_iota(jnp.int32, ends.shape, 1)
        ends = jnp.round(ends * jnp.where(at_row < 4, *edge_factors))
        messages[at, slabs * rows :, :] = to_int16(
            jnp.concatenate([ends.reshape(slabs * 4, LANES), *edge_codes, code], axis=0)
        )
        tops[:, 0, :] = factor

        def code_slab(slab, _):
            messages[at, rows_of(slab), :] = to_int16(jnp.round(values[rows_of(slab), :] * tops[slab, 0:1, :]))
            return 0

        lax.fori_loop(0, slabs, code_slab, 0, unroll=2)
        for i, out in enumerate(outs):

            @pl.when(at == i)
            def _():
                pltpu.make_async_copy(messages.at[i], out, out_sems.at[i]).start()

        return 0

    lax.fori_loop(0, count, one_partner, 0)
    for i, out in enumerate(outs):
        pltpu.make_async_copy(messages.at[i], out, out_sems.at[i]).wait()


def split_kernel(a_ref, both_ref):
    a = a_ref[...]
    size = a.shape[-1]
    hi = a.astype(jnp.bfloat16)
    both_ref[:, :, size:] = hi
    both_ref[:, :, :size] = (a - hi.astype(jnp.float32)).astype(jnp.bfloat16)


def swapped(edges):
    return jnp.concatenate([edges[1:2], edges[0:1], edges[3:4], edges[2:3]], axis=0)


def product_kernel(order, first_slab, slabs, lower_slabs, pair_ref, edge_weight, *refs):
    groups = len(order)
    ins, both_ref = refs[:groups], refs[groups]
    outs, scratch, all_codes = refs[-groups - 9 : -9], refs[-9:-1], refs[-1]
    size = both_ref.shape[1]
    levels = size // (2 * groups)
    rows = 2 * levels
    me = lax.axis_index("rad")
    pair = pair_ref[0]
    peers = [lax.bitwise_xor(me, k) for k in order]
    near = lax.broadcasted_iota(jnp.int32, (8, LANES), 0)

    def place(f, peer):
        return pl.ds(pl.multiple_of(f * (size // 2) + peer * levels, levels), levels)

    def one_tile(t):
        v_both, y, edges, codes = scratch[t % 2 * 4 : t % 2 * 4 + 4]
        extras = []
        for ref, peer in zip(ins, peers):
            extra = to_float(ref[slabs * rows :, :])
            power = jnp.exp2(extra[4 * slabs :] * (1.0 / FINE))
            extras.append(power[slabs + 2 * t : slabs + 2 * t + 2] * (1.0 / TOP))
            for j in range(2):
                at = t * 8 + j * 4
                code = j * (slabs // 2) + t
                edges[peer, :, j * LANES : (j + 1) * LANES] = extra[at : at + 4] * (
                    power[code : code + 1] * (1.0 / EDGE_TOP)
                )
        for ref, peer, scales in zip(ins, peers, extras):
            before, after = jnp.maximum(peer - 1, 0), jnp.minimum(peer + 1, groups - 1)
            weight_before, weight_after = edge_weight[peer], edge_weight[groups + peer]
            for j in range(2):
                cols = slice(j * LANES, (j + 1) * LANES)
                scale = scales[j : j + 1]
                here = swapped(edges[peer, :, cols])
                low = weight_before * (edges[before, :, cols] - here)
                high = weight_after * (edges[after, :, cols] - here)
                start = (t * 2 + j) * rows
                for f in range(2):
                    v = to_float(ref[start + f * levels : start + (f + 1) * levels, :]) * scale
                    first = v[:8] + jnp.where(near == 0, low[2 * f + 1 : 2 * f + 2], 0.0)
                    last = v[levels - 8 :] + jnp.where(near == 7, high[2 * f : 2 * f + 1], 0.0)
                    middle = [v[8 : levels - 8]] if levels > 16 else []
                    v = jnp.concatenate([first] + middle + [last], axis=0)
                    hi = v.astype(jnp.bfloat16)
                    v_both[place(f, peer), cols] = hi
                    v_both[place(f + 2, peer), cols] = (v - hi.astype(jnp.float32)).astype(jnp.bfloat16)

        def product(which):
            dot = functools.partial(jnp.dot, preferred_element_type=jnp.float32)
            return dot(both_ref[which], v_both[...]) + dot(both_ref[which, :, size:], v_both[:size, :])

        upper = product(1)
        if first_slab + t < lower_slabs:
            lane = lax.broadcasted_iota(jnp.int32, upper.shape, 1)
            column = (first_slab + t) * LANES + jnp.where(lane < LANES, lane, lane - LANES + 1)
            y[...] = jnp.where(column < pair + 1, product(0), upper)
        else:
            y[...] = upper

        def results(peer, j):
            return jnp.concatenate([y[place(f, peer), j * LANES : (j + 1) * LANES] for f in range(2)], axis=0)

        for i, peer in enumerate(peers):
            for j in range(2):
                v = jnp.abs(results(peer, j))
                codes[j, i] = jnp.max(v.reshape(rows // 8, 8, LANES), axis=0)
        code = scale_code(jnp.max(codes[...], axis=2), FINE)
        factor = encode_factor(code, TOP)
        for i, (out, peer) in enumerate(zip(outs, peers)):
            for j in range(2):
                start = (t * 2 + j) * rows
                out[start : start + rows, :] = to_int16(
                    jnp.round(results(peer, j) * factor[j, i : i + 1])
                )
                all_codes[i, t * 2 + j : t * 2 + j + 1, :] = code[j, i : i + 1]

    all_codes[...] = jnp.zeros_like(all_codes)
    for t in range(slabs // 2):
        one_tile(t)
    for i, out in enumerate(outs):
        out[slabs * rows :, :] = to_int16(all_codes[i])


def result_kernel(ks, slabs, skipped, width, *refs):
    count = len(ks)
    ins, (out_ref, buffer, sems) = refs[:count], refs[-3:]
    levels = out_ref.shape[1]
    rows = 2 * levels
    span = slabs // 2 * LANES
    copies = []
    for at, (message, k) in enumerate(zip(ins, ks)):
        scales = scale_of(to_float(message[slabs * rows :, :]), TOP)
        first_col = lax.bitwise_xor(lax.axis_index("rad"), k) * width + skipped
        for half in range(2):
            for pair in range(slabs // 2):
                slab = pair * 2 + half
                for f in range(2):
                    start = slab * rows + f * levels
                    v = to_float(message[start : start + levels, :])
                    buffer[at, half, f, :, pair * LANES : (pair + 1) * LANES] = v * scales[slab : slab + 1, :]
            cols = pl.ds(pl.multiple_of(first_col + half * (width // 2), LANES), span)
            copies.append(pltpu.make_async_copy(buffer.at[at, half], out_ref.at[:, :, cols], sems.at[at, half]))
            copies[-1].start()
    for copy in copies:
        copy.wait()


def send(message, k, groups):
    return message if k == 0 else lax.ppermute(message, "rad", [(i, i ^ k) for i in range(groups)])


def local(slots, nonlin, state, inverse, pair_of_slot):
    levels = nonlin.shape[1]
    groups = lax.axis_size("rad")
    width = nonlin.shape[2] // groups
    size = inverse.shape[-1]
    all_slabs = width // LANES
    half_cols = width // 2
    span = half_cols // CHUNKS
    slabs = 2 * span // LANES
    rows = 2 * levels
    lower_slabs = -(-slots // LANES)
    weights = stencil_table(levels * groups)
    table = jnp.asarray(weights)
    edge_weight = jnp.asarray(np.concatenate([weights[::levels, 0], weights[levels - 1 :: levels, 2]]))
    vmem = pl.BlockSpec(memory_space=pltpu.VMEM)
    hbm = pl.BlockSpec(memory_space=pl.ANY)
    far = list(range(groups // 2, groups))
    near = list(range(groups // 2))
    others = near[1:]
    order = []
    for i, k in enumerate(far):
        order += [k] + others[2 * i : 2 * i + 2]
    order += near[:1]

    def call(kernel, name, flops, moved, vmem_mib, **kwargs):
        return pl.pallas_call(
            kernel,
            name=name,
            compiler_params=pltpu.CompilerParams(vmem_limit_bytes=vmem_mib * MIB),
            cost_estimate=pl.CostEstimate(flops=flops, bytes_accessed=moved, transcendentals=0),
            **kwargs,
        )

    def right_side(ks, chunk, *earlier):
        out_rows = slabs * (rows + EXTRA)
        count = len(ks)
        return call(
            functools.partial(right_side_kernel, ks, slabs, chunk * span, width),
            "right_side",
            MIB * count,
            MIB * count,
            56,
            out_shape=[jax.ShapeDtypeStruct((out_rows, LANES), jnp.int16)] * count,
            in_specs=[hbm] * (3 + len(earlier)),
            out_specs=[hbm] * count,
            scratch_shapes=[
                pltpu.VMEM((count, 2, 2, levels, span), jnp.bfloat16),
                pltpu.VMEM((count, 2, 2, levels, span), jnp.float32),
                pltpu.VMEM((levels, LANES), jnp.float32),
                pltpu.VMEM((count, out_rows, LANES), jnp.int16),
                pltpu.VMEM((slabs * rows, LANES), jnp.float32),
                pltpu.VMEM((slabs, 8, LANES), jnp.float32),
                pltpu.VMEM((slabs // 2, 8, LANES), jnp.float32),
                pltpu.SemaphoreType.DMA((count, 2, 2)),
                pltpu.SemaphoreType.DMA((count + 1,)),
            ],
        )(nonlin, state, table, *earlier)

    def split():
        block = pl.BlockSpec((1, size // 4, size), lambda i, j: (i, j, 0))
        return call(
            split_kernel,
            "split_inverse",
            4 * MIB,
            16 * MIB,
            16,
            out_shape=jax.ShapeDtypeStruct((2, size, 2 * size), jnp.bfloat16),
            grid=(2, 4),
            in_specs=[block],
            out_specs=pl.BlockSpec((1, size // 4, 2 * size), lambda i, j: (i, j, 0)),
        )(inverse[0])

    def product(chunk, messages, both, *earlier):
        return call(
            functools.partial(product_kernel, order, chunk * span // LANES, slabs, lower_slabs),
            "product",
            6 * size * size * slabs * LANES,
            10 * MIB,
            32,
            out_shape=[jax.ShapeDtypeStruct((slabs * rows + CODES, LANES), jnp.int16)] * groups,
            in_specs=[pl.BlockSpec(memory_space=pltpu.SMEM)] * 2
            + [vmem] * (groups + 1)
            + [hbm for _ in earlier],
            out_specs=[vmem] * groups,
            scratch_shapes=2
            * [
                pltpu.VMEM((2 * size, 2 * LANES), jnp.bfloat16),
                pltpu.VMEM((size, 2 * LANES), jnp.float32),
                pltpu.VMEM((groups, 4, 2 * LANES), jnp.float32),
                pltpu.VMEM((2, groups, 8, LANES), jnp.float32),
            ]
            + [pltpu.VMEM((groups, CODES, LANES), jnp.float32)],
        )(pair_of_slot, edge_weight, *messages, both, *earlier)

    def result(ks, chunk, messages, previous):
        carried = [] if previous is None else [previous]
        return call(
            functools.partial(result_kernel, ks, slabs, chunk * span, width),
            "result",
            MIB,
            2 * MIB,
            16,
            out_shape=jax.ShapeDtypeStruct(state.shape, jnp.float32),
            in_specs=[vmem] * len(messages) + [hbm] * len(carried),
            out_specs=hbm,
            scratch_shapes=[
                pltpu.VMEM((len(ks), 2, 2, levels, span), jnp.float32),
                pltpu.SemaphoreType.DMA((len(ks), 2)),
            ],
            input_output_aliases={} if previous is None else {len(ks): 0},
        )(*messages, *carried)

    made, got = [], {}
    for ks, chunk in ((far[:2], 0), (near + far[2:], 0), (far + near, 1)):
        made = right_side(ks, chunk, *made[-1:])
        got.update({(k, chunk): send(m, k, groups) for k, m in zip(ks, made)})
    both = split()
    back, made = [], []
    for chunk in range(CHUNKS):
        made = product(chunk, [got[k, chunk] for k in order], both, *made[-1:])
        back.append({k: send(m, k, groups) for k, m in zip(order, made)})
    out = None
    for chunk, came in enumerate(back):
        for ks in [order] if chunk < CHUNKS - 1 else [order[:4] + order[-1:], order[4:-1]]:
            out = result(ks, chunk, [came[k] for k in ks], out)
    return out


def solution(mesh):
    placed = (
        P(None, "rad", "ang"),
        P(None, "rad", "ang"),
        P(("ang", "rad"), None, None, None),
        P(("ang", "rad")),
    )
    slots = mesh.shape["rad"] * mesh.shape["ang"]
    return jax.shard_map(
        functools.partial(local, slots),
        mesh=mesh,
        in_specs=placed,
        out_specs=P(None, "rad", "ang"),
        check_vma=False,
    )
```
